128 devices in a mesh: gx: 8 (over x, core), gy: 16 (over z, y).
Axes of the slice: x: 4, y: 4, z: 4, core: 2. Of those that a mesh axis runs over, the one named last changes fastest.
Arguments:
- enthalpy: float32 [160, 256, 1024], P(None, 'gy', 'gx'), may hold values from -6 to 6
- conduct_col: float32 [256, 1024], P('gy', 'gx'), may hold values from 0.5 to 40
- conduct_level: float32 [160], replicated, may hold values from 1 to 16
- surface_enthalpy: float32 [256, 1024], P('gy', 'gx'), may hold values from -6 to 6
- geothermal: float32 [256, 1024], P('gy', 'gx'), may hold values from 0.1 to 1
- melt_level: float32 [256, 1024], P('gy', 'gx'), may hold values from 0 to 0.5
- viscosity: float32 [256, 1024], P('gy', 'gx'), may hold values from 0.5 to 5
- drag: float32 [256, 1024], P('gy', 'gx'), may hold values from 0.05 to 0.5
- driving_stress: float32 [2, 256, 1024], P(None, 'gy', 'gx')
- ice_mask: int32 [256, 1024], P('gy', 'gx'), may hold values 0 or 1
- basin: int32 [256, 1024], P('gy', 'gx'), may hold values from 0 to 255, as said below
- owner_slot: int32 [256], replicated, may hold values from 0 to 255, each once
Outputs:
- enthalpy_next: float32 [160, 256, 1024], P(None, 'gy', 'gx')
- velocity: float32 [2, 256, 1024], P(None, 'gy', 'gx')
- basin_melt: float32 [256], P(('gx', 'gy'))
The draws below stay inside these ranges and needn't reach their ends.
Inputs may be any that keep to these rules, and one draw needn't show every extreme that they name: `basin`: constant on aligned tiles of 32 x 32 columns; every basin holds the same number of tiles. `owner_slot`: each slot once.
All inputs are finite; a program needn't handle non-finite values. No bound on the sum of `ice_mask` on one device may be relied on, other than what follows from the above.
Results may differ from the reference program's by a relative error of at most 0.00028.
Values sent between devices are 32-bit elements; how exact they have to be, the bound alone decides.
No kernel may reach another device: no remote copies, remote signals or barrier semaphores. Data moves between devices by JAX's collectives and lax.ppermute only.
A program may use at most 128 MiB of HBM per device.

```python
import math
import jax
import jax.numpy as jnp
from jax import lax

NZ = 160
ITERS = 3
ADV_STEPS = 8
TILE = 32
NX = 1024
NY = 256
BASINS = 256
N_GY = 16


def draw_driving_stress(key, part):
    key = jax.random.fold_in(key, 11)
    ramp_x = 1.0 + 2.0 * jnp.arange(NX, dtype=jnp.float32) / (NX - 1)
    values = jax.random.normal(key, (2, NY, NX), jnp.float32) + 0.4
    return values * ramp_x[None, None, :]


def draw_basin(key, part):
    key = jax.random.fold_in(key, 5)
    tiles_y = NY // TILE
    tiles_x = NX // TILE
    order = jax.random.permutation(key, tiles_y * tiles_x)
    tile_basin = (order % BASINS).reshape(tiles_y, tiles_x).astype(jnp.int32)
    return jnp.repeat(jnp.repeat(tile_basin, TILE, axis=0), TILE, axis=1)


def with_ends(values, key, smallest, top_value):
    extent = values.shape
    index_at = [jax.random.randint(jax.random.fold_in(key, axis), (), 0, extent[axis]) for axis in range(len(extent))]
    values = values.at[tuple(index_at)].set(smallest)
    longest = extent.index(max(extent))
    index_at[longest] = (index_at[longest] + 1) % extent[longest]
    return values.at[tuple(index_at)].set(top_value)


def shard_levels(key, shape, pieces, low, largest):
    factor_of = 1.0
    for dim, shards_of in pieces:
        steps = jax.random.uniform(jax.random.fold_in(jax.random.fold_in(key, 6), dim), (shards_of,), jnp.float32, low / len(pieces), largest / len(pieces))
        factor_of = factor_of * jnp.repeat(jnp.exp(steps), shape[dim] // shards_of).reshape((-1,) + (1,) * (len(shape) - 1 - dim))
    return factor_of


def normal_values(rng, shape, deviation, bound, pieces=(), held_as=jnp.bfloat16):
    values = jax.random.normal(rng, shape, jnp.float32) * deviation
    if len(pieces) > 0:
        values = shard_levels(rng, shape, pieces, -0.22, 0.18) * values
    return jnp.clip(values, min=-bound, max=bound).astype(held_as)


def setup_inputs(seed: int = 0) -> dict:
    arg_keys = jax.random.split(jax.random.key(seed), 13)
    enthalpy = normal_values(arg_keys[0], (NZ, NY, NX), 1.0, 6.0, ((1, 16), (2, 8)), jnp.float32)
    conduct_col = jnp.clip(jnp.exp(math.log(40.0) - 4.3820266 * jax.random.uniform(arg_keys[1], (NY, NX), jnp.float32) ** shard_levels(arg_keys[1], (NY, NX), ((0, 16), (1, 8)), -0.2, 0.2)), 0.5, 40.0)
    conduct_level = jnp.clip(jnp.exp(jax.random.uniform(arg_keys[2], (NZ,), jnp.float32, math.log(1.0), math.log(16.0))), 1.0, 16.0)
    surface_enthalpy = normal_values(arg_keys[3], (NY, NX), 1.0, 6.0, ((0, 16), (1, 8)), jnp.float32)
    geothermal = jnp.clip(jnp.exp(math.log(1.0) - 2.3025851 * jax.random.uniform(arg_keys[4], (NY, NX), jnp.float32) ** shard_levels(arg_keys[4], (NY, NX), ((0, 16), (1, 8)), -0.2, 0.2)), 0.1, 1.0)
    melt_level = jnp.clip(0.5 * jax.random.uniform(arg_keys[5], (NY, NX), jnp.float32) ** shard_levels(arg_keys[5], (NY, NX), ((0, 16), (1, 8)), -0.2, 0.2), 0.0, 0.5)
    viscosity = jnp.clip(jnp.exp(math.log(5.0) - 2.3025851 * jax.random.uniform(arg_keys[6], (NY, NX), jnp.float32) ** shard_levels(arg_keys[6], (NY, NX), ((0, 16), (1, 8)), -0.2, 0.2)), 0.5, 5.0)
    drag = jnp.clip(jnp.exp(math.log(0.5) - 2.3025851 * jax.random.uniform(arg_keys[7], (NY, NX), jnp.float32) ** shard_levels(arg_keys[7], (NY, NX), ((0, 16), (1, 8)), -0.2, 0.2)), 0.05, 0.5)
    driving_stress = draw_driving_stress(jax.random.fold_in(arg_keys[12], 71), 0)
    ice_mask = with_ends((jax.random.randint(arg_keys[9], (NY, NX), 0, 5) < 4).astype(jnp.int32), jax.random.fold_in(arg_keys[9], 1), 0, 1)
    basin = draw_basin(jax.random.fold_in(arg_keys[12], 71), 0)
    owner_slot = jax.random.permutation(arg_keys[11], BASINS).astype(jnp.int32)
    return {"enthalpy": enthalpy, "conduct_col": conduct_col, "conduct_level": conduct_level, "surface_enthalpy": surface_enthalpy, "geothermal": geothermal, "melt_level": melt_level, "viscosity": viscosity, "drag": drag, "driving_stress": driving_stress, "ice_mask": ice_mask, "basin": basin, "owner_slot": owner_slot}


def face_terms(viscosity, padded, drag):
    east = 0.5 * (viscosity + padded[1:-1, 2:])
    west = 0.5 * (viscosity + padded[1:-1, :-2])
    north = 0.5 * (viscosity + padded[2:, 1:-1])
    south = 0.5 * (viscosity + padded[:-2, 1:-1])
    center = drag + east + west + north + south
    return center, east, west, north, south


def apply_faces(field, padded, faces):
    center, east, west, north, south = faces
    result = center * field - east * padded[:, 1:-1, 2:] - west * padded[:, 1:-1, :-2]
    return result - north * padded[:, 2:, 1:-1] - south * padded[:, :-2, 1:-1]


def upwind(padded, courant_x, courant_y):
    middle = padded[..., 1:-1, 1:-1]
    western = padded[..., 1:-1, :-2]
    eastern = padded[..., 1:-1, 2:]
    southern = padded[..., :-2, 1:-1]
    northern = padded[..., 2:, 1:-1]
    result = middle - jnp.maximum(courant_x, 0.0) * (middle - western) - jnp.minimum(courant_x, 0.0) * (eastern - middle)
    return result - jnp.maximum(courant_y, 0.0) * (middle - southern) - jnp.minimum(courant_y, 0.0) * (northern - middle)


def level_profile(levels):
    height = (jnp.arange(levels, dtype=jnp.float32) + 0.5) / levels
    return 1.0 - (1.0 - height) ** 4


def thomas_solve(below_coef, diagonal, above_coef, right_side):
    def forward(carry, items):
        prev_ratio, prev_value = carry
        below, middle, above, source = items
        pivot = middle - below * prev_ratio
        ratio = above / pivot
        value = (source + below * prev_value) / pivot
        return (ratio, value), (ratio, value)

    start = jnp.zeros_like(right_side[0])
    _, (ratios, values) = lax.scan(forward, (start, start), (below_coef, diagonal, above_coef, right_side), unroll=8)

    def backward(upper_value, items):
        ratio, value = items
        result = value + ratio * upper_value
        return result, result

    _, solved = lax.scan(backward, start, (ratios, values), reverse=True, unroll=8)
    return solved


def column_step(advected, conduct_col, conduct_level, bottom, surface):
    diffusion = conduct_col[None] * conduct_level[:, None, None]
    zero_row = jnp.zeros_like(diffusion[:1])
    below_coef = jnp.concatenate([zero_row, diffusion[:-1]], axis=0)
    above_coef = jnp.concatenate([diffusion[:-1], zero_row], axis=0)
    diagonal = 1.0 + below_coef + diffusion
    right_side = jnp.concatenate([advected[:1] + bottom[None], advected[1:-1], advected[-1:] + diffusion[-1:] * surface[None]], axis=0)
    return thomas_solve(below_coef, diagonal, above_coef, right_side)


def reference(enthalpy, conduct_col, conduct_level, surface_enthalpy, geothermal, melt_level, viscosity, drag, driving_stress, ice_mask, basin, owner_slot):
    faces = face_terms(viscosity, jnp.pad(viscosity, 1), drag)

    def operate(field):
        return apply_faces(field, jnp.pad(field, ((0, 0), (1, 1), (1, 1))), faces)

    velocity = jnp.zeros_like(driving_stress)
    residual = driving_stress
    direction = driving_stress
    norm_now = jnp.sum(residual * residual)
    for step in range(ITERS):
        image = operate(direction)
        alpha = norm_now / jnp.sum(direction * image)
        velocity = velocity + alpha * direction
        residual = residual - alpha * image
        norm_next = jnp.sum(residual * residual)
        direction = residual + (norm_next / norm_now) * direction
        norm_now = norm_next

    profile = level_profile(NZ)

    def advect_level(items):
        level, factor = items
        courant_x = 0.45 * jnp.tanh(3.0 * velocity[0] * factor)
        courant_y = 0.45 * jnp.tanh(3.0 * velocity[1] * factor)
        for step in range(ADV_STEPS):
            level = upwind(jnp.pad(level, 1), courant_x, courant_y)
        return level

    advected = lax.map(advect_level, (enthalpy, profile))
    bottom = geothermal + 10.0 * drag * (velocity[0] * velocity[0] + velocity[1] * velocity[1])
    blocks = N_GY
    rows = NY // blocks

    def split3(field):
        return jnp.transpose(field.reshape(NZ, blocks, rows, NX), (1, 0, 2, 3))

    def solve_block(items):
        adv_block, col_block, bottom_block, surface_block = items
        return column_step(adv_block, col_block, conduct_level, bottom_block, surface_block)

    solved = lax.map(solve_block, (split3(advected), conduct_col.reshape(blocks, rows, NX), bottom.reshape(blocks, rows, NX), surface_enthalpy.reshape(blocks, rows, NX)))
    solved = jnp.transpose(solved, (1, 0, 2, 3)).reshape(NZ, NY, NX)
    enthalpy_next = jnp.where(ice_mask[None] == 1, solved, enthalpy)
    melt = jnp.where(ice_mask == 1, jnp.maximum(solved[0] - melt_level, 0.0), 0.0)
    totals = jax.ops.segment_sum(melt.reshape(-1), basin.reshape(-1), num_segments=BASINS)
    slots = jnp.zeros((BASINS,), dtype=melt.dtype).at[owner_slot].set(totals)
    basin_melt = slots * (BASINS / (NX * NY))
    return enthalpy_next, velocity, basin_melt
```

```python
import functools

import jax
import jax.numpy as jnp
from jax import lax
from jax.experimental import pallas as pl
from jax.experimental.pallas import tpu as pltpu
from jax.sharding import PartitionSpec as P

STEPS = 8
NZ = 160
ROWS = 16
LANES = 128
GROUPS = NZ // 8
SCALE = 16.0
SLOT = 24
BYTES = 48 * 1024 * 1024


def lane_ids(shape):
    return lax.broadcasted_iota(jnp.int32, shape, len(shape) - 1)


def row_ids(shape):
    return lax.broadcasted_iota(jnp.int32, shape, len(shape) - 2)


def turn(x, shift, axis):
    shift = shift % x.shape[axis]
    return x if shift == 0 else pltpu.roll(x, shift, axis)


def call(kernel, outs, *args, smem=(), scratch=(), flops=0):
    specs = [
        pl.BlockSpec(memory_space=pltpu.SMEM if i in smem else pltpu.VMEM)
        for i in range(len(args))
    ]
    size = sum(a.size * 4 for a in args) + sum(o.size * 4 for o in outs)
    return pl.pallas_call(
        kernel,
        out_shape=outs,
        in_specs=specs,
        out_specs=[pl.BlockSpec(memory_space=pltpu.VMEM)] * len(outs),
        scratch_shapes=list(scratch),
        compiler_params=pltpu.CompilerParams(vmem_limit_bytes=BYTES),
        cost_estimate=pl.CostEstimate(
            flops=flops, bytes_accessed=size, transcendentals=0
        ),
    )(*args)


def f32(*shape):
    return jax.ShapeDtypeStruct(shape, jnp.float32)


def stencil(visc, drag, keep_e, keep_w, keep_n, keep_s):
    wide = visc.shape[1]
    tall = visc.shape[0]
    east = 0.5 * (visc + turn(visc, -1, 1) * keep_e)
    west = 0.5 * (visc + turn(visc, 1, 1) * keep_w)
    north = 0.5 * (visc + turn(visc, -1, 0) * keep_n)
    south = 0.5 * (visc + turn(visc, 1, 0) * keep_s)
    center = drag + east + west + north + south
    inv = 1.0 / SCALE
    center, east, west, north, south = (
        center * inv,
        east * keep_e * inv,
        west * keep_w * inv,
        north * keep_n * inv,
        south * keep_s * inv,
    )

    def apply(w):
        return (
            center * w
            - east * turn(w, -1, 1)
            - west * turn(w, 1, 1)
            - north * turn(w, -1, 0)
            - south * turn(w, 1, 0)
        )

    return apply


def pack_first_columns(f_ref, y_ref, o_ref):
    lane = lane_ids((8, LANES))
    out = jnp.zeros((8, LANES), jnp.float32)
    for f in range(4):
        for t in range(3):
            x = y_ref[f] if t == 2 else f_ref[f, 8 * t : 8 * t + 8, :]
            at = (3 * f + t) * 8
            out = jnp.where((lane >= at) & (lane < at + 8), turn(x, at, 1), out)
    o_ref[...] = out


def moments_kernel(f_ref, y_ref, x_ref, at_ref, o_ref):
    lane8 = lane_ids((8, LANES))
    fields = []
    for f in range(4):
        main = jnp.concatenate([f_ref[f], y_ref[f]], axis=0)
        extra = []
        for t in range(3):
            piece = turn(x_ref[...], -(3 * f + t) * 8, 1)
            extra.append(jnp.where(lane8 < 8, piece, 0.0))
        fields.append(jnp.concatenate([main, jnp.concatenate(extra, axis=0)], axis=1))
    shape = fields[0].shape
    lane, row = lane_ids(shape), row_ids(shape)
    last_x = jnp.where(at_ref[0] == 7, 127, -9)
    last_y = jnp.where(at_ref[1] == 15, 15, -9)
    keep_e = jnp.where(lane == last_x, 0.0, 1.0)
    keep_w = jnp.where(lane == last_x + 1, 0.0, 1.0)
    keep_n = jnp.where(row == last_y, 0.0, 1.0)
    keep_s = jnp.where(row == last_y + 1, 0.0, 1.0)
    apply = stencil(fields[2], fields[3], keep_e, keep_w, keep_n, keep_s)
    inside = (row >= 3) & (row < 19) & (lane >= 3) & (lane < 131)
    v0 = fields[:2]
    v1 = [apply(w) for w in v0]
    v2 = [apply(w) for w in v1]
    v3 = [apply(w) for w in v2]
    result = jnp.zeros((1, LANES), jnp.float32)
    pairs = ((v0, v0), (v0, v1), (v1, v1), (v1, v2), (v2, v2), (v2, v3))
    for j, (p, q) in enumerate(pairs):
        prod = jnp.where(inside, p[0] * q[0] + p[1] * q[1], 0.0)
        part = prod[:, :LANES] + prod[:, LANES:]
        total = jnp.sum(jnp.sum(part, axis=0, keepdims=True), axis=1, keepdims=True)
        result = jnp.where(lane_ids((1, LANES)) == j, total, result)
    o_ref[...] = jnp.broadcast_to(result, (LANES, LANES))


def level_rows(e_ref, s_ref, n_ref, g, y):
    if y < 8:
        return s_ref[pl.ds(g * 64 + y, 8, stride=8), :]
    if y < 24:
        return e_ref[pl.ds(g * 128 + (y - 8), 8, stride=16), :]
    return n_ref[pl.ds(g * 64 + (y - 24), 8, stride=8), :]


def payload_place(g, y):
    if g < 16:
        return y, g * 8
    return 32 + y // 4, ((y % 4) * 4 + (g - 16)) * 8


def field_tile(f_ref, s_ref, n_ref, f, t):
    if t < 2:
        at = (NZ + 2 * f + t) * 8
        return s_ref[at : at + 8, :]
    if t < 4:
        return f_ref[f, 8 * (t - 2) : 8 * (t - 2) + 8, :]
    at = (NZ + 2 * f + t - 4) * 8
    return n_ref[at : at + 8, :]


def pack_columns(e_ref, f_ref, s_ref, n_ref, first_ref, last_ref):
    lane = lane_ids((8, LANES))
    zero = jnp.zeros((8, LANES), jnp.float32)
    tiles = {}

    def put(tile, at, width, x):
        first, last = tiles.get(tile, (zero, zero))
        here = (lane >= at) & (lane < at + width)
        first = jnp.where(here, turn(x, at, 1), first)
        last = jnp.where(here, turn(x, at + width - LANES, 1), last)
        tiles[tile] = (first, last)

    def flush(tile):
        first, last = tiles.pop(tile)
        first_ref[8 * tile : 8 * tile + 8, :] = first
        last_ref[8 * tile : 8 * tile + 8, :] = last

    for y in range(32):
        for g in range(GROUPS):
            tile, at = payload_place(g, y)
            put(tile, at, 8, level_rows(e_ref, s_ref, n_ref, g, y))
        flush(y)
        if y % 4 == 3:
            flush(32 + y // 4)
    for i in range(24):
        put(40 + i // 8, (i % 8) * 16, 16, field_tile(f_ref, s_ref, n_ref, i // 6, i % 6))
        if i % 8 == 7:
            flush(40 + i // 8)


def build_strips(e_ref, s_ref, n_ref, w_ref, x_ref, o_ref):
    lane = lane_ids((8, LANES))
    for y in range(32):
        for t in range(4):
            west = jnp.zeros((8, LANES), jnp.float32)
            east = west
            for j in range(5):
                g = 5 * t + j
                own = level_rows(e_ref, s_ref, n_ref, g, y)
                tile, at = payload_place(g, y)
                base = SLOT * j
                halo_w = w_ref[8 * tile : 8 * tile + 8, :]
                halo_e = x_ref[8 * tile : 8 * tile + 8, :]
                outer = (lane >= base) & (lane < base + 8)
                inner = (lane >= base + 8) & (lane < base + SLOT)
                west = jnp.where(outer, turn(halo_w, base - at, 1), west)
                west = jnp.where(inner, turn(own, base + 8, 1), west)
                inner = (lane >= base) & (lane < base + 16)
                outer = (lane >= base + 16) & (lane < base + SLOT)
                east = jnp.where(inner, turn(own, base - 112, 1), east)
                east = jnp.where(outer, turn(halo_e, base + 16 - at, 1), east)
            at = (t * 32 + y) * 8
            o_ref[at : at + 8, :] = west
            at = ((t + 4) * 32 + y) * 8
            o_ref[at : at + 8, :] = east


def basis_kernel(f_ref, s_ref, n_ref, w_ref, x_ref, at_ref, o_ref):
    lane8 = lane_ids((8, LANES))
    fields = []
    for f in range(4):
        main, extra = [], []
        for t in range(6):
            main.append(field_tile(f_ref, s_ref, n_ref, f, t))
            i = 6 * f + t
            tile = 40 + i // 8
            east = turn(x_ref[8 * tile : 8 * tile + 8, :], -(i % 8) * 16, 1)
            west = turn(w_ref[8 * tile : 8 * tile + 8, :], 112 - (i % 8) * 16, 1)
            extra.append(jnp.where(lane8 < 16, east, jnp.where(lane8 >= 112, west, 0.0)))
        fields.append(
            jnp.concatenate(
                [jnp.concatenate(main, axis=0), jnp.concatenate(extra, axis=0)], axis=1
            )
        )
    shape = fields[0].shape
    lane, row = lane_ids(shape), row_ids(shape)
    low_y = jnp.where(at_ref[1] == 0, 16, 0)
    high_y = jnp.where(at_ref[1] == 15, 32, 48)
    end_x = jnp.where(at_ref[0] == 7, 128, 144)
    start_x = jnp.where(at_ref[0] == 0, 256, 240)
    inside = (row >= low_y) & (row < high_y) & ((lane < end_x) | (lane >= start_x))
    inside = jnp.where(inside, 1.0, 0.0)
    apply = stencil(fields[2], fields[3], 1.0, 1.0, 1.0, 1.0)
    vectors = [fields[:2]]
    for _ in range(2):
        vectors.append([apply(w) * inside for w in vectors[-1]])
    lane32 = lane_ids((32, LANES))
    for b in range(3):
        for c in range(2):
            v = vectors[b][c][8:40, :]
            o_ref[0, c, b] = v[:, :LANES]
            for side, shift in ((1, 8), (2, -112)):
                one = turn(v, shift, 1)[:, :LANES]
                one = jnp.where(lane32 < SLOT, one, 0.0)
                rep = one
                for j in range(1, 5):
                    rep = rep + turn(one, SLOT * j, 1)
                o_ref[side, c, b] = rep


def pivots_kernel(col_ref, lev_ref, basin_ref, owner_ref, inv_ref, slot_ref):
    col = col_ref[...]

    def step(i, s):
        k = NZ - 2 - i
        r = col * lev_ref[k]
        at = pl.multiple_of((k + 1) * ROWS, ROWS)
        inv_ref[pl.ds(at, ROWS), :] = 1.0 / (s + r)
        return 1.0 + r * (s / (s + r))

    s = lax.fori_loop(0, NZ - 1, step, 1.0 + col * lev_ref[NZ - 1], unroll=3)
    inv_ref[0:ROWS, :] = 1.0 / s
    basin = basin_ref[0:1, :]
    lane = lane_ids((1, LANES))
    owner = owner_ref[...]
    ids = row_ids(owner.shape) * LANES + lane_ids(owner.shape)
    for j in range(4):
        mine = jnp.sum(jnp.where(lane == 32 * j, basin, 0), axis=1, keepdims=True)
        slot = jnp.where(ids == mine, owner, 0)
        slot = jnp.sum(jnp.sum(slot, axis=0, keepdims=True), axis=1, keepdims=True)
        slot_ref[8 * j : 8 * j + 8, :] = jnp.broadcast_to(slot, (8, LANES))


def cg_coefficients(m):
    a0 = m[0] / m[1]
    rr1 = a0 * a0 * m[2] - m[0]
    b0 = rr1 / m[0]
    p1 = (1.0 + b0, -a0)
    q1 = p1[0] * p1[0] * m[1] + 2.0 * p1[0] * p1[1] * m[2] + p1[1] * p1[1] * m[3]
    a1 = rr1 / q1
    r2 = (1.0, -a0 - a1 * p1[0], -a1 * p1[1])

    def form(p, k):
        return (
            p[0] * p[0] * m[k]
            + 2.0 * p[0] * p[1] * m[k + 1]
            + (2.0 * p[0] * p[2] + p[1] * p[1]) * m[k + 2]
            + 2.0 * p[1] * p[2] * m[k + 3]
            + p[2] * p[2] * m[k + 4]
        )

    rr2 = form(r2, 0)
    b1 = rr2 / rr1
    p2 = (1.0 + b1 * p1[0], r2[1] + b1 * p1[1], r2[2])
    a2 = rr2 / form(p2, 1)
    inv = 1.0 / SCALE
    return (
        (a0 + a1 * p1[0] + a2 * p2[0]) * inv,
        (a1 * p1[1] + a2 * p2[1]) * inv,
        a2 * p2[2] * inv,
    )


def main_kernel(
    e_ref, s_ref, n_ref, strip_ref, basis_ref, sums_ref, inv_ref, col_ref, lev_ref,
    geo_ref, drag_ref, surf_ref, melt_ref, mask_ref, slot_ref,
    g_ref, vel_ref, send_ref,
    flow, cour, done, adv,
):
    lane8 = lane_ids((8, LANES))
    total = jnp.sum(sums_ref[...], axis=0, keepdims=True)
    lane1 = lane_ids((1, LANES))
    m = [
        jnp.sum(jnp.where(lane1 == j, total, 0.0), axis=1, keepdims=True) for j in range(6)
    ]
    c = [jnp.broadcast_to(x, (32, LANES)) for x in cg_coefficients(m)]
    for kind in range(3):
        for comp in range(2):
            v = c[0] * basis_ref[kind, comp, 0]
            v = v + c[1] * basis_ref[kind, comp, 1]
            v = v + c[2] * basis_ref[kind, comp, 2]
            if kind == 0:
                vel_ref[comp] = v[8:24]
            for y in range(1, 31):
                flow[kind, comp, y] = jnp.broadcast_to(v[y : y + 1], (8, LANES))

    def profile(k):
        height = (k.astype(jnp.float32) + 0.5) / NZ
        low = 1.0 - height
        low = low * low
        return 1.0 - low * low

    def courants(kind, prof, slot):
        for comp in range(2):
            for y in range(1, 31):
                cour[slot, comp, y] = 0.45 * jnp.tanh(3.0 * flow[kind, comp, y] * prof)

    def transport(kind, loads, stores, skew):
        tiles = range(len(loads))
        state = [{} for _ in tiles]
        for d in range(32 + skew * STEPS):
            if d < 32:
                for i in tiles:
                    state[i][0, d] = loads[i](d)
            for s in range(STEPS, 0, -1) if skew > 1 else range(1, STEPS + 1):
                y = d - skew * s
                if not s <= y <= 31 - s:
                    continue
                east_flow = flow[kind, 0, y] > 0.0
                north_flow = flow[kind, 1, y] > 0.0
                for i in tiles:
                    now = state[i][s - 1, y]
                    side = jnp.where(east_flow, turn(now, 1, 1), turn(now, -1, 1))
                    other = jnp.where(
                        north_flow, state[i][s - 1, y - 1], state[i][s - 1, y + 1]
                    )
                    new = (
                        now
                        - jnp.abs(cour[i, 0, y]) * (now - side)
                        - jnp.abs(cour[i, 1, y]) * (now - other)
                    )
                    if s == STEPS:
                        stores[i](y, new)
                    else:
                        state[i][s, y] = new

    PAIR = 2

    for kind in (1, 2):
        def strip_body(q, carry, kind=kind):
            loads, stores = [], []
            for i in range(PAIR):
                t = q * PAIR + i
                tile = (kind - 1) * 4 + t
                seg = jnp.zeros((8, LANES), jnp.int32)
                for j in range(1, 5):
                    seg = seg + jnp.where(lane8 >= SLOT * j, 1, 0)
                k = (t * 5 + seg) * 8 + row_ids((8, LANES))
                courants(kind, profile(k), i)

                def load(y, tile=tile):
                    at = pl.multiple_of(tile * 256 + y * 8, 8)
                    return strip_ref[pl.ds(at, 8), :]

                def store(y, x, tile=tile):
                    at = pl.multiple_of(tile * 128 + (y - 8) * 8, 8)
                    done[pl.ds(at, 8), :] = x

                loads.append(load)
                stores.append(store)
            transport(kind, loads, stores, 2)
            return carry

        lax.fori_loop(0, 4 // PAIR, strip_body, 0)

    col = col_ref[...]

    def group_body(q, above):
        loads, stores = [], []
        first = GROUPS - PAIR - q * PAIR
        for i in range(PAIR):
            g = first + i
            courants(0, profile(g * 8 + row_ids((8, LANES))), i)
            t = g // 5
            j = g - 5 * t

            def load(y, g=g):
                return level_rows(e_ref, s_ref, n_ref, g, y)

            def store(y, x, i=i, t=t, j=j):
                at = pl.multiple_of(t * 128 + (y - 8) * 8, 8)
                west = pltpu.roll(done[pl.ds(at, 8), :], 120 - SLOT * j, 1)
                at = pl.multiple_of((t + 4) * 128 + (y - 8) * 8, 8)
                east = pltpu.roll(done[pl.ds(at, 8), :], 112 - SLOT * j, 1)
                x = jnp.where(lane8 < 8, west, jnp.where(lane8 >= 120, east, x))
                adv[pl.ds(i * 128 + y - 8, 8, stride=16), :] = x

            loads.append(load)
            stores.append(store)
        transport(0, loads, stores, 2)
        for i in range(8 * PAIR - 1, -1, -1):
            k = first * 8 + i
            inv = inv_ref[pl.ds(pl.multiple_of(k * ROWS, ROWS), ROWS), :]
            weight = col * lev_ref[k] * inv
            above = adv[i * 16 : i * 16 + 16, :] * inv + weight * above
            g_ref[pl.ds(pl.multiple_of(k * ROWS, ROWS), ROWS), :] = above
        return above

    solved = lax.fori_loop(0, GROUPS // PAIR, group_body, surf_ref[...])
    u, v = vel_ref[0], vel_ref[1]
    bottom = geo_ref[...] + 10.0 * drag_ref[...] * (u * u + v * v)
    solved = solved + bottom * inv_ref[0:ROWS, :]
    g_ref[0:ROWS, :] = solved
    melt = jnp.where(mask_ref[...] == 1, jnp.maximum(solved - melt_ref[...], 0.0), 0.0)
    melt = jnp.sum(melt, axis=0, keepdims=True)
    place = row_ids((LANES, LANES)) * 2 + lane_ids((LANES, LANES))
    place = jnp.where(lane_ids((LANES, LANES)) < 2, place, -1)
    out = jnp.zeros((LANES, LANES), jnp.float32)
    for j in range(4):
        part = jnp.where((lane1 >= 32 * j) & (lane1 < 32 * j + 32), melt, 0.0)
        part = jnp.sum(part, axis=1, keepdims=True)
        slot = slot_ref[8 * j : 8 * j + 1, :]
        out = out + jnp.where(place == slot, part, 0.0)
    send_ref[...] = out


def back_kernel(g_ref, inv_ref, col_ref, lev_ref, e_ref, mask_ref, o_ref):
    col = col_ref[...]
    ice = mask_ref[...] == 1

    def put(k, x):
        at = pl.ds(pl.multiple_of(k * ROWS, ROWS), ROWS)
        o_ref[at, :] = jnp.where(ice, x, e_ref[at, :])

    below = g_ref[0:ROWS, :]
    put(0, below)

    def step(k, below):
        at = pl.ds(pl.multiple_of(k * ROWS, ROWS), ROWS)
        below = g_ref[at, :] + col * lev_ref[k - 1] * inv_ref[at, :] * below
        put(k, below)
        return below

    lax.fori_loop(1, NZ, step, below, unroll=3)


def per_device(
    enthalpy,
    conduct_col,
    conduct_level,
    surface_enthalpy,
    geothermal,
    melt_level,
    viscosity,
    drag,
    driving_stress,
    ice_mask,
    basin,
    owner_slot,
):
    nx, ny = lax.axis_size("gx"), lax.axis_size("gy")
    both = ("gx", "gy")
    at = jnp.stack([lax.axis_index("gx"), lax.axis_index("gy")]).astype(jnp.int32)
    fields = jnp.concatenate([driving_stress, viscosity[None], drag[None]])
    flat = enthalpy.reshape(NZ * ROWS, LANES)

    with jax.named_scope("moments"):
        ring_y = [((i + 1) % ny, i) for i in range(ny)]
        ring_x = [((i + 1) % nx, i) for i in range(nx)]
        rows = lax.ppermute(fields[:, :8], "gy", ring_y)
        (message,) = call(pack_first_columns, [f32(8, LANES)], fields, rows)
        columns = lax.ppermute(message, "gx", ring_x)
        (sums,) = call(
            moments_kernel, [f32(LANES, LANES)], fields, rows, columns, at, smem=(3,)
        )
        sums = lax.all_to_all(sums.reshape(LANES, 1, LANES), both, 0, 0)
        sums = sums.reshape(LANES, LANES)

    with jax.named_scope("halo_rows"):
        up_y = [(i, i + 1) for i in range(ny - 1)]
        down_y = [(i + 1, i) for i in range(ny - 1)]
        tiles = fields.reshape(8, 8, LANES)
        upper = jnp.concatenate([enthalpy[:, 8:], tiles])
        lower = jnp.concatenate([enthalpy[:, :8], tiles])
        south = lax.ppermute(upper, "gy", up_y).reshape(-1, LANES)
        north = lax.ppermute(lower, "gy", down_y).reshape(-1, LANES)

    with jax.named_scope("halo_columns"):
        up_x = [(i, i + 1) for i in range(nx - 1)]
        down_x = [(i + 1, i) for i in range(nx - 1)]
        first, last = call(
            pack_columns, [f32(43 * 8, LANES)] * 2, flat, fields, south, north
        )
        west = lax.ppermute(last, "gx", up_x)
        east = lax.ppermute(first, "gx", down_x)

    with jax.named_scope("prepare"):
        inv, slots = call(
            pivots_kernel,
            [f32(NZ * ROWS, LANES), jax.ShapeDtypeStruct((32, LANES), jnp.int32)],
            conduct_col, conduct_level, basin, owner_slot.reshape(2, LANES),
            smem=(1,),
        )
        (strips,) = call(
            build_strips, [f32(8 * 32 * 8, LANES)], flat, south, north, west, east
        )
        (basis,) = call(
            basis_kernel, [f32(3, 2, 3, 32, LANES)], fields, south, north, west, east, at,
            smem=(5,),
        )

    with jax.named_scope("transport"):
        reduced, velocity, send = call(
            main_kernel,
            [f32(NZ * ROWS, LANES), f32(2, ROWS, LANES), f32(LANES, LANES)],
            flat, south, north, strips, basis, sums, inv, conduct_col, conduct_level,
            geothermal, drag, surface_enthalpy, melt_level, ice_mask, slots,
            smem=(8,),
            scratch=(
                pltpu.VMEM((3, 2, 32, 8, LANES), jnp.float32),
                pltpu.VMEM((2, 2, 32, 8, LANES), jnp.float32),
                pltpu.VMEM((8 * 16 * 8, LANES), jnp.float32),
                pltpu.VMEM((256, LANES), jnp.float32),
            ),
        )

    with jax.named_scope("basin_melt"):
        received = lax.all_to_all(send.reshape(LANES, 1, LANES), both, 0, 0)
        owned = jnp.sum(received.reshape(LANES, LANES)[:, :2], axis=0)
        count = owner_slot.shape[0]
        basin_melt = owned * (count / (ROWS * LANES * nx * ny))

    with jax.named_scope("substitution"):
        (solved,) = call(
            back_kernel, [f32(NZ * ROWS, LANES)],
            reduced, inv, conduct_col, conduct_level, flat, ice_mask,
            smem=(3,),
        )
    return (solved.reshape(NZ, ROWS, LANES), velocity, basin_melt)


def solution(mesh):
    return jax.shard_map(
        per_device,
        mesh=mesh,
        in_specs=(
            P(None, "gy", "gx"),
            P("gy", "gx"),
            P(),
            P("gy", "gx"),
            P("gy", "gx"),
            P("gy", "gx"),
            P("gy", "gx"),
            P("gy", "gx"),
            P(None, "gy", "gx"),
            P("gy", "gx"),
            P("gy", "gx"),
            P(),
        ),
        out_specs=(P(None, "gy", "gx"), P(None, "gy", "gx"), P(("gx", "gy"))),
        check_vma=False,
    )
```

```python
import jax
import jax.numpy as jnp
from jax import lax
from jax.experimental import pallas as pl
from jax.experimental.pallas import tpu as pltpu
from jax.sharding import PartitionSpec as P

STEPS = 8
NZ = 160
ROWS = 16
LANES = 128
GROUPS = NZ // 8
SCALE = 16.0
WIDE = 144
BAND = 48
FULL = 60


def lane_ids(shape):
    return lax.broadcasted_iota(jnp.int32, shape, len(shape) - 1)


def row_ids(shape):
    return lax.broadcasted_iota(jnp.int32, shape, len(shape) - 2)


def turn(x, shift, axis):
    shift = shift % x.shape[axis]
    return x if shift == 0 else pltpu.roll(x, shift, axis)


def f32(*shape):
    return jax.ShapeDtypeStruct(shape, jnp.float32)


def call(kernel, outs, *args, places, scratch=(), limit=8, flops=0, aliases={}):
    spaces = {"v": pltpu.VMEM, "s": pltpu.SMEM, "a": pltpu.HBM}
    specs = [
        pl.BlockSpec(memory_space=spaces[p]) if p in spaces else pl.BlockSpec()
        for p in places
    ]
    size = sum(a.size * 4 for a in args) + sum(o.size * 4 for o in outs)
    return pl.pallas_call(
        kernel,
        out_shape=outs,
        in_specs=specs[: len(args)],
        out_specs=specs[len(args) :],
        scratch_shapes=list(scratch),
        input_output_aliases=aliases,
        compiler_params=pltpu.CompilerParams(vmem_limit_bytes=limit * 1024 * 1024),
        cost_estimate=pl.CostEstimate(
            flops=flops, bytes_accessed=size, transcendentals=0
        ),
    )(*args)


def rows_at(start, size):
    return pl.ds(pl.multiple_of(start, size if size in (8, 16) else 8), size)


def stencil(visc, drag, keep_e, keep_w, keep_n, keep_s):
    wide = visc.shape[1]
    tall = visc.shape[0]
    east = 0.5 * (visc + turn(visc, -1, 1) * keep_e)
    west = 0.5 * (visc + turn(visc, 1, 1) * keep_w)
    north = 0.5 * (visc + turn(visc, -1, 0) * keep_n)
    south = 0.5 * (visc + turn(visc, 1, 0) * keep_s)
    center = drag + east + west + north + south
    inv = 1.0 / SCALE
    center, east, west, north, south = (
        center * inv,
        east * keep_e * inv,
        west * keep_w * inv,
        north * keep_n * inv,
        south * keep_s * inv,
    )

    def apply(w):
        return (
            center * w
            - east * turn(w, -1, 1)
            - west * turn(w, 1, 1)
            - north * turn(w, -1, 0)
            - south * turn(w, 1, 0)
        )

    return apply


def edge_tile(tiles, first):
    lane = lane_ids((8, LANES))
    out = jnp.zeros((8, LANES), jnp.float32)
    for i in range(8):
        x = turn(tiles[i], 16 * i if first else 16 * i - 112, 1)
        out = jnp.where((lane >= 16 * i) & (lane < 16 * i + 16), x, out)
    return out


def fetch_all(pairs, sems):
    copies = [
        pltpu.make_async_copy(src, dst, sems.at[i]) for i, (src, dst) in enumerate(pairs)
    ]
    for copy in copies:
        copy.start()
    return copies


def wait_all(copies):
    for copy in copies:
        copy.wait()


def fields_kernel(stress_ref, visc_ref, drag_ref, f_ref, raw, out, sems):
    pairs = [(stress_ref, raw.at[pl.ds(0, 2)]), (visc_ref, raw.at[2]), (drag_ref, raw.at[3])]
    wait_all(fetch_all(pairs, sems))
    tiles = [raw[i // 2, 8 * (i % 2) : 8 * (i % 2) + 8, :] for i in range(8)]
    for i in range(8):
        out[i] = tiles[i]
    out[8] = edge_tile(tiles, True)
    out[9] = edge_tile(tiles, False)
    wait_all(fetch_all([(out, f_ref)], sems))


def transpose_kernel(
    e_ref, f_ref, lo_ref, hi_ref, first_ref, last_ref,
    buf, out, first, last, in_sems, out_sems,
):
    loads = [
        pltpu.make_async_copy(e_ref.at[:, pl.ds(8 * h, 8), :], buf.at[h], in_sems.at[h])
        for h in range(2)
    ]
    for copy in loads:
        copy.start()
    edges = fetch_all(
        [(f_ref.at[8], first.at[32]), (f_ref.at[9], last.at[32])], out_sems
    )
    wait_all(edges)
    stores = []
    for h, o_ref in ((0, lo_ref), (1, hi_ref)):
        loads[h].wait()
        for y in range(8):
            tiles = [buf[h, 8 * g : 8 * g + 8, y, :] for g in range(GROUPS)]
            wide = jnp.concatenate(tiles[:16], axis=0).T
            upper = jnp.concatenate(tiles[16:], axis=0)
            bands = jnp.concatenate([turn(upper, -32 * q, 1) for q in range(4)], axis=0)
            bands = bands.T[:32, :]
            out[h, y, :LANES, :] = wide
            out[h, y, LANES:, :] = bands
            first[8 * h + y] = wide[:8]
            last[8 * h + y] = wide[120:]
            first[16 + 8 * h + y] = bands[:8]
            last[16 + 8 * h + y] = bands[24:]
        dst = o_ref.at[:, pl.ds(0, NZ), :]
        copy = pltpu.make_async_copy(out.at[h], dst, out_sems.at[h])
        copy.start()
        stores.append(copy)
    for i, (a, b) in enumerate(((first, first_ref), (last, last_ref))):
        copy = pltpu.make_async_copy(a, b.at[pl.ds(0, 33)], out_sems.at[2 + i])
        copy.start()
        stores.append(copy)
    for copy in stores:
        copy.wait()


LOW = 192
HIGH = 208


def corners_kernel(
    lo_in, hi_in, f_hbm, w_hbm, x_hbm, lo_ref, hi_ref, fields, west, east, sems, out_sems
):
    del lo_in, hi_in
    loads = fetch_all([(w_hbm, west), (x_hbm, east), (f_hbm, fields)], sems)
    pairs = []
    for o_ref, base in ((lo_ref, 0), (hi_ref, 8)):
        for i, ref in enumerate((west, east)):
            for part in range(2):
                src = ref.at[pl.ds(16 * part + base, 8)]
                pairs.append((src, o_ref.at[:, pl.ds(160 + 16 * part + 8 * i, 8), :]))
    pairs.append((fields.at[pl.ds(0, 8)], hi_ref.at[:, pl.ds(192, 8), :]))
    pairs.append((west.at[32], hi_ref.at[0, pl.ds(200, 8), :]))
    pairs.append((east.at[32], hi_ref.at[1, pl.ds(200, 8), :]))
    wait_all(loads)
    wait_all(fetch_all(pairs, out_sems))


def edges_kernel(first_in, last_in, y_ref, first_ref, last_ref, sems):
    del first_in, last_in
    pairs = [(y_ref.at[8], first_ref.at[33]), (y_ref.at[9], last_ref.at[33])]
    wait_all(fetch_all(pairs, sems))


def moments_kernel(f_hbm, y_hbm, x_hbm, o_ref, f_ref, y_ref, x_ref, out, sems):
    pairs = [(f_hbm, f_ref), (y_hbm, y_ref), (x_hbm.at[pl.ds(32, 2)], x_ref)]
    wait_all(fetch_all(pairs, sems))
    lane8 = lane_ids((8, LANES))
    fields = []
    for f in range(4):
        main = jnp.concatenate([f_ref[2 * f], f_ref[2 * f + 1], y_ref[2 * f]], axis=0)
        extra = [
            turn(x_ref[0], -16 * (2 * f), 1),
            turn(x_ref[0], -16 * (2 * f + 1), 1),
            turn(x_ref[1], -16 * (2 * f), 1),
        ]
        extra = [jnp.where(lane8 < 16, x, 0.0) for x in extra]
        fields.append(jnp.concatenate([main, jnp.concatenate(extra, axis=0)], axis=1))
    shape = fields[0].shape
    lane, row = lane_ids(shape), row_ids(shape)
    last_x = jnp.where(lax.axis_index("gx") == 7, 127, -9)
    last_y = jnp.where(lax.axis_index("gy") == 15, 15, -9)
    keep_e = jnp.where(lane == last_x, 0.0, 1.0)
    keep_w = jnp.where(lane == last_x + 1, 0.0, 1.0)
    keep_n = jnp.where(row == last_y, 0.0, 1.0)
    keep_s = jnp.where(row == last_y + 1, 0.0, 1.0)
    apply = stencil(fields[2], fields[3], keep_e, keep_w, keep_n, keep_s)
    inside = (row >= 3) & (row < 19) & (lane >= 3) & (lane < 131)
    v0 = fields[:2]
    v1 = [apply(w) for w in v0]
    v2 = [apply(w) for w in v1]
    v3 = [apply(w) for w in v2]
    result = jnp.zeros((1, LANES), jnp.float32)
    pairs = ((v0, v0), (v0, v1), (v1, v1), (v1, v2), (v2, v2), (v2, v3))
    for j, (p, q) in enumerate(pairs):
        prod = jnp.where(inside, p[0] * q[0] + p[1] * q[1], 0.0)
        part = prod[:, :LANES] + prod[:, LANES:]
        total = jnp.sum(jnp.sum(part, axis=0, keepdims=True), axis=1, keepdims=True)
        result = jnp.where(lane_ids((1, LANES)) == j, total, result)
    out[...] = jnp.broadcast_to(result, (LANES, LANES))
    wait_all(fetch_all([(out, o_ref)], sems))


def basis_kernel(
    f_ref, w_ref, x_ref, s_ref, y_ref, o_hbm, t_hbm,
    own, west, east, south, s_w, s_e, north, o_ref, t_ref, sems,
):
    pairs = (
        (f_ref, own), (w_ref.at[pl.ds(32, 2)], west), (x_ref.at[pl.ds(32, 2)], east),
        (s_ref.at[:, pl.ds(192, 8), :], south), (s_ref.at[0, pl.ds(200, 8), :], s_w),
        (s_ref.at[1, pl.ds(200, 8), :], s_e), (y_ref, north),
    )
    wait_all(fetch_all(pairs, sems))
    lane8 = lane_ids((8, LANES))
    fields = []
    for f in range(4):
        main, extra = [], []
        for t in range(6):
            i = 2 * f + t % 2
            if t < 2:
                mid, left, right = south[i], s_w[...], s_e[...]
            elif t < 4:
                mid, left, right = own[i], west[0], east[0]
            else:
                mid, left, right = north[i], west[1], east[1]
            main.append(mid)
            right = turn(right, -16 * i, 1)
            left = turn(left, 112 - 16 * i, 1)
            extra.append(jnp.where(lane8 < 16, right, jnp.where(lane8 >= 112, left, 0.0)))
        fields.append(
            jnp.concatenate(
                [jnp.concatenate(main, axis=0), jnp.concatenate(extra, axis=0)], axis=1
            )
        )
    shape = fields[0].shape
    lane, row = lane_ids(shape), row_ids(shape)
    low_y = jnp.where(lax.axis_index("gy") == 0, 16, 0)
    high_y = jnp.where(lax.axis_index("gy") == 15, 32, 48)
    end_x = jnp.where(lax.axis_index("gx") == 7, 128, 144)
    start_x = jnp.where(lax.axis_index("gx") == 0, 256, 240)
    inside = (row >= low_y) & (row < high_y) & ((lane < end_x) | (lane >= start_x))
    inside = jnp.where(inside, 1.0, 0.0)
    fields = [x * inside for x in fields]
    apply = stencil(fields[2], fields[3], 1.0, 1.0, 1.0, 1.0)
    vectors = [fields[:2]]
    for _ in range(2):
        vectors.append([apply(w) * inside for w in vectors[-1]])
    fill = jnp.zeros((96, LANES), jnp.float32)
    for b in range(3):
        for c in range(2):
            v = vectors[b][c]
            o_ref[c, b] = v[16:32, :LANES]
            v = turn(v[8:40, :], 8, 1)
            t_ref[c, b, :LANES] = jnp.concatenate([v[:, :LANES], fill], axis=0).T
            t_ref[c, b, LANES:] = jnp.concatenate([v[:, LANES:], fill], axis=0).T[:16, :]
    wait_all(fetch_all([(o_ref, o_hbm), (t_ref, t_hbm)], sems))


def pivots_kernel(
    col_ref, lev_ref, basin_ref, owner_ref, geo_ref, drag_ref, surf_ref, melt_ref, mask_ref,
    inv_ref, plane_ref, inv, planes, basin, owner, mask, plane, sems, out_sems,
):
    pairs = [
        (col_ref, planes.at[4]), (basin_ref, basin), (owner_ref, owner), (mask_ref, mask),
        (geo_ref, planes.at[0]), (drag_ref, planes.at[1]), (surf_ref, planes.at[2]),
        (melt_ref, planes.at[3]),
    ]
    wait_all(fetch_all(pairs, sems))
    col = planes[4]

    def step(i, s):
        k = NZ - 1 - i
        lower = col * lev_ref[k - 1]
        one = 1.0 / (s + lower)
        inv[rows_at(k * ROWS, ROWS), :] = one
        return 1.0 + lower * (s * one)

    s = 1.0 + col * lev_ref[NZ - 1]
    stores = []
    for part, (a, b) in enumerate(((0, 80), (80, NZ - 1))):
        s = lax.fori_loop(a, b, step, s, unroll=16)
        if part == 1:
            inv[0:ROWS, :] = 1.0 / s
        at = pl.ds((1 - part) * 80 * ROWS, 80 * ROWS)
        stores.append(pltpu.make_async_copy(inv.at[at], inv_ref.at[at], out_sems.at[part]))
        stores[-1].start()
    for i in range(4):
        plane[16 * i : 16 * i + 16, :] = planes[i]
    plane[64:80, :] = jnp.where(mask[...] == 1, 1.0, 0.0)
    lane = lane_ids((1, LANES))
    slots = owner[...]
    ids = row_ids(slots.shape) * LANES + lane_ids(slots.shape)
    for j in range(4):
        mine = jnp.sum(jnp.where(lane == 32 * j, basin[0:1, :], 0), axis=1, keepdims=True)
        slot = jnp.where(ids == mine, slots, 0)
        slot = jnp.sum(jnp.sum(slot, axis=0, keepdims=True), axis=1, keepdims=True)
        slot = slot.astype(jnp.float32)
        plane[80 + 8 * j : 88 + 8 * j, :] = jnp.broadcast_to(slot, (8, LANES))
    plane[112:128, :] = col
    stores.append(pltpu.make_async_copy(plane, plane_ref, out_sems.at[2]))
    stores[-1].start()
    wait_all(stores)


def cg_coefficients(m):
    a0 = m[0] / m[1]
    rr1 = a0 * a0 * m[2] - m[0]
    b0 = rr1 / m[0]
    p1 = (1.0 + b0, -a0)
    q1 = p1[0] * p1[0] * m[1] + 2.0 * p1[0] * p1[1] * m[2] + p1[1] * p1[1] * m[3]
    a1 = rr1 / q1
    r2 = (1.0, -a0 - a1 * p1[0], -a1 * p1[1])

    def form(p, k):
        return (
            p[0] * p[0] * m[k]
            + 2.0 * p[0] * p[1] * m[k + 1]
            + (2.0 * p[0] * p[2] + p[1] * p[1]) * m[k + 2]
            + 2.0 * p[1] * p[2] * m[k + 3]
            + p[2] * p[2] * m[k + 4]
        )

    rr2 = form(r2, 0)
    b1 = rr2 / rr1
    p2 = (1.0 + b1 * p1[0], r2[1] + b1 * p1[1], r2[2])
    a2 = rr2 / form(p2, 1)
    inv = 1.0 / SCALE
    return (
        (a0 + a1 * p1[0] + a2 * p2[0]) * inv,
        (a1 * p1[1] + a2 * p2[1]) * inv,
        a2 * p2[2] * inv,
    )


def main_kernel(
    lo_ref, hi_ref, s_ref, n_ref, w_ref, x_ref,
    basis_ref, turned_ref, sums_ref, inv_ref, plane_ref, lev_ref,
    g_ref, vel_ref, send_ref,
    wide, band, wide_x, wide_y, band_x, band_y, flow, adv,
    west_b, east_b, basis, turned, sums, inv, plane, lev, solved, vel, send,
    sems, out_sems,
):
    lane8 = lane_ids((8, LANES))
    lane1 = lane_ids((1, LANES))
    copies = []

    def fetch(src, dst):
        copy = pltpu.make_async_copy(src, dst, sems.at[len(copies)])
        copy.start()
        copies.append(copy)
        return copy

    sums_here = fetch(sums_ref, sums)
    turned_here = fetch(turned_ref, turned)
    basis_here = fetch(basis_ref, basis)
    field_here = []
    for i, ref in enumerate((s_ref, lo_ref, hi_ref, n_ref)):
        y = pl.ds(8 * i, 8)
        field_here.append(fetch(ref.at[:, pl.ds(0, 128), :], wide.at[0, y, pl.ds(16, 128), :]))
        field_here.append(fetch(ref.at[:, pl.ds(128, 32), :], band.at[0, y, pl.ds(16, 32), :]))
    for at, x, ref in ((160, 8, w_ref), (168, 144, x_ref)):
        for y, msg in ((0, s_ref), (24, n_ref)):
            dst = wide.at[0, pl.ds(y, 8), pl.ds(x, 8), :]
            field_here.append(fetch(msg.at[:, pl.ds(at, 8), :], dst))
        dst = wide.at[0, pl.ds(8, 16), pl.ds(x, 8), :]
        field_here.append(fetch(ref.at[pl.ds(0, 16)], dst))
    for at, buf, ref in ((176, west_b, w_ref), (184, east_b, x_ref)):
        field_here.append(fetch(s_ref.at[:, pl.ds(at, 8), :], buf.at[pl.ds(0, 8)]))
        field_here.append(fetch(ref.at[pl.ds(16, 16)], buf.at[pl.ds(8, 16)]))
        field_here.append(fetch(n_ref.at[:, pl.ds(at, 8), :], buf.at[pl.ds(24, 8)]))
    later = [fetch(inv_ref, inv), fetch(lev_ref, lev), fetch(plane_ref, plane)]

    sums_here.wait()
    total = jnp.sum(sums[...], axis=0, keepdims=True)
    m = [
        jnp.sum(jnp.where(lane1 == j, total, 0.0), axis=1, keepdims=True) for j in range(6)
    ]
    c = cg_coefficients(m)

    def profile(k):
        height = (k.astype(jnp.float32) + 0.5) / NZ
        low = 1.0 - height
        low = low * low
        return 1.0 - low * low

    prof_w = profile(lane8)
    prof_b = profile(128 + lane8 % 32)
    turned_here.wait()

    def courants(i, carry):
        for j in range(6):
            at = rows_at((i * 6 + j) * 8, 8)
            for comp, o_ref in ((0, wide_x), (1, wide_y)):
                v = c[0] * turned[comp, 0, at, :]
                v = v + c[1] * turned[comp, 1, at, :]
                v = v + c[2] * turned[comp, 2, at, :]
                v = 3.0 * v
                for y in range(1, 31):
                    one = jnp.broadcast_to(v[:, y : y + 1], (8, LANES))
                    flow[comp, y, at, :] = one
                    o_ref[y, at, :] = 0.45 * jnp.tanh(one * prof_w)
        return carry

    lax.fori_loop(0, 3, courants, 0)

    def band_courants(i, carry):
        for j in range(3):
            t = i * 3 + j
            for comp, o_ref in ((0, band_x), (1, band_y)):
                for y in range(1, 31):
                    one = flow[comp, y, rows_at(t * 8, 8), :]
                    for q in range(1, 4):
                        other = flow[comp, y, rows_at(t * 8 + 32 * q, 8), :]
                        one = jnp.where(lane8 >= 32 * q, other, one)
                    o_ref[y, rows_at(t * 8, 8), :] = 0.45 * jnp.tanh(one * prof_b)
        return carry

    lax.fori_loop(0, 2, band_courants, 0)

    basis_here.wait()
    for comp in range(2):
        v = c[0] * basis[comp, 0] + c[1] * basis[comp, 1] + c[2] * basis[comp, 2]
        vel[comp] = v
    vel_out = pltpu.make_async_copy(vel, vel_ref, out_sems.at[0])
    vel_out.start()

    for copy in field_here:
        copy.wait()
    keep = jnp.where(lax.axis_index("gx") == 7, 0.0, 1.0)
    for y in range(32):
        wide[0, y, 144:152, :] = wide[0, y, 144:152, :] * keep
        left = turn(band[0, y, 40:48, :], 32, 1)
        left = jnp.where(lane8 < 32, turn(west_b[y], 32, 1), left)
        right = turn(band[0, y, 16:24, :], 96, 1)
        right = jnp.where(lane8 >= 96, turn(east_b[y] * keep, 96, 1), right)
        band[0, y, 8:16, :] = left
        band[0, y, 48:56, :] = right

    def substep(buf, cx_ref, cy_ref, s, t):
        src, dst = (s - 1) % 2, s % 2
        at = pl.multiple_of(t * 8, 8)
        mid = pl.ds(at + 8, 8)

        now = buf[src, s, mid, :]
        below = now - buf[src, s - 1, mid, :]
        for y in range(s, 32 - s):
            above = buf[src, y + 1, mid, :]
            west = buf[src, y, pl.ds(at + 7, 8), :]
            east = buf[src, y, pl.ds(at + 9, 8), :]
            cx = cx_ref[y, pl.ds(at, 8), :]
            cy = cy_ref[y, pl.ds(at, 8), :]
            rise = above - now
            across = jnp.where(cx > 0.0, now - west, east - now)
            along = jnp.where(cy > 0.0, below, rise)
            buf[dst, y, mid, :] = now - cx * across - cy * along
            now, below = above, rise

    for s in range(1, STEPS + 1):
        last = s == STEPS

        def tiles(i, carry, s=s, last=last):
            for j in range(8 if last else 6):
                t = i * 8 + j + 1 if last else i * 6 + j
                substep(wide, wide_x, wide_y, s, t)
            for j in range(2):
                substep(band, band_x, band_y, s, i * 2 + j + (1 if last else 0))
            return carry

        lax.fori_loop(0, 2 if last else 3, tiles, 0)

    def back(i, carry):
        for j in range(4):
            y = i * 4 + j
            x = wide[0, y + 8, 16:144, :].T
            for g in range(16):
                adv[pl.ds(g * 128 + y, 8, stride=16), :] = x[8 * g : 8 * g + 8, :]
        x = jnp.concatenate([band[0, i * 4 + j + 8, 16:48, :] for j in range(4)], axis=0).T
        for g in range(4):
            for j in range(4):
                out = None
                for q in range(4):
                    one = x[32 * q + 8 * g : 32 * q + 8 * g + 8, :]
                    one = turn(one, 32 * (q - j), 1)
                    out = one if q == 0 else jnp.where(lane8 >= 32 * q, one, out)
                adv[pl.ds((16 + g) * 128 + i * 4 + j, 8, stride=16), :] = out
        return carry

    lax.fori_loop(0, 4, back, 0)

    for copy in later:
        copy.wait()

    col = plane[112:128, :]

    def eliminate(i, above):
        k = NZ - 1 - i
        at = rows_at(k * ROWS, ROWS)
        one = inv[at, :]
        above = adv[at, :] * one + col * lev[k] * one * above
        solved[at, :] = above
        return above

    outs = [vel_out]
    parts = 5
    size = NZ // parts
    above = plane[32:48, :]
    for part in range(parts):
        above = lax.fori_loop(part * size, (part + 1) * size, eliminate, above, unroll=16)
        if part == parts - 1:
            u, v = vel[0], vel[1]
            bottom = plane[0:16, :] + 10.0 * plane[16:32, :] * (u * u + v * v)
            above = above + bottom * inv[0:ROWS, :]
            solved[0:ROWS, :] = above
        at = pl.ds((NZ - (part + 1) * size) * ROWS, size * ROWS)
        copy = pltpu.make_async_copy(solved.at[at], g_ref.at[at], out_sems.at[1 + part])
        copy.start()
        outs.append(copy)

    melt = jnp.where(plane[64:80, :] == 1.0, jnp.maximum(above - plane[48:64, :], 0.0), 0.0)
    melt = jnp.sum(melt, axis=0, keepdims=True) * MEAN
    place = row_ids((LANES, LANES)) * 2 + lane_ids((LANES, LANES))
    place = jnp.where(lane_ids((LANES, LANES)) < 2, place, -1).astype(jnp.float32)
    out = jnp.zeros((LANES, LANES), jnp.float32)
    for j in range(4):
        part = jnp.where((lane1 >= 32 * j) & (lane1 < 32 * j + 32), melt, 0.0)
        part = jnp.sum(part, axis=1, keepdims=True)
        slot = plane[80 + 8 * j : 81 + 8 * j, :]
        out = out + jnp.where(place == slot, part, 0.0)
    send[...] = out
    copy = pltpu.make_async_copy(send, send_ref, out_sems.at[1 + parts])
    copy.start()
    outs.append(copy)
    for copy in outs:
        copy.wait()


def back_kernel(g_ref, inv_ref, e_ref, mask_ref, plane_ref, lev_ref, o_ref):
    col = plane_ref[112:128, :]
    ice = mask_ref[...] == 1

    def step(k, below):
        at = rows_at(k * ROWS, ROWS)
        below = g_ref[at, :] + col * lev_ref[k - 1] * inv_ref[at, :] * below
        o_ref[at, :] = jnp.where(ice, below, e_ref[at, :])
        return below

    below = g_ref[0:ROWS, :]
    o_ref[0:ROWS, :] = jnp.where(ice, below, e_ref[0:ROWS, :])
    lax.fori_loop(1, NZ, step, below, unroll=16)


MEAN = 256 / 262144


def per_device(
    enthalpy,
    conduct_col,
    conduct_level,
    surface_enthalpy,
    geothermal,
    melt_level,
    viscosity,
    drag,
    driving_stress,
    ice_mask,
    basin,
    owner_slot,
):
    nx, ny = lax.axis_size("gx"), lax.axis_size("gy")
    both = ("gx", "gy")
    up_x = [(i, i + 1) for i in range(nx - 1)]
    ring_x = [((i + 1) % nx, i) for i in range(nx)]
    up_y = [(i, i + 1) for i in range(ny - 1)]
    down_y = [(i + 1, i) for i in range(ny - 1)]
    ring_y = [((i + 1) % ny, i) for i in range(ny)]
    dma = pltpu.SemaphoreType.DMA

    def vmem(*shape, dtype=jnp.float32):
        return pltpu.VMEM(shape, dtype)

    tie = lax.optimization_barrier

    with jax.named_scope("fields"):
        (fields,) = call(
            fields_kernel, [f32(10, 8, LANES)], driving_stress, viscosity, drag,
            places="aaa" + "a",
            scratch=(vmem(4, ROWS, LANES), vmem(10, 8, LANES), dma((3,))),
            limit=FULL,
        )
        rows = lax.ppermute(fields, "gy", ring_y)
    with jax.named_scope("levels_on_lanes"):
        low, high, first, last = call(
            transpose_kernel,
            [f32(8, LOW, LANES), f32(8, HIGH, LANES)] + [f32(34, 8, LANES)] * 2,
            enthalpy, fields, places="aa" + "aaaa",
            scratch=(
                vmem(2, NZ, 8, LANES), vmem(2, 8, NZ, LANES),
                vmem(33, 8, LANES), vmem(33, 8, LANES), dma((2,)), dma((4,)),
            ),
            limit=FULL,
        )
        first, last = call(
            edges_kernel, [f32(34, 8, LANES)] * 2, first, last, rows, places="aaa" + "aa",
            scratch=(dma((2,)),), limit=FULL, aliases={0: 0, 1: 1},
        )
    with jax.named_scope("moments"):
        east = lax.ppermute(first, "gx", ring_x)
        west = lax.ppermute(last, "gx", up_x)
        (sums,) = call(
            moments_kernel, [f32(LANES, LANES)], fields, rows, east, places="aaa" + "a",
            scratch=(
                vmem(10, 8, LANES), vmem(10, 8, LANES), vmem(2, 8, LANES),
                vmem(LANES, LANES), dma((3,)),
            ),
            limit=FULL,
        )

    with jax.named_scope("halo"):
        low, high = call(
            corners_kernel, [f32(8, LOW, LANES), f32(8, HIGH, LANES)],
            low, high, fields, west, east, places="aaaaa" + "aa",
            scratch=(
                vmem(10, 8, LANES), vmem(34, 8, LANES), vmem(34, 8, LANES), dma((3,)), dma((11,)),
            ),
            limit=FULL, aliases={0: 0, 1: 1},
        )
        south = lax.ppermute(high, "gy", up_y)
        north = lax.ppermute(low, "gy", down_y)

    with jax.named_scope("moments"):
        every = lax.all_to_all(sums.reshape(LANES, 1, LANES), both, 0, 0)
        every = every.reshape(LANES, LANES)

    with jax.named_scope("prepare"):
        late_col, _ = tie((conduct_col, sums))
        inv, plane = call(
            pivots_kernel,
            [f32(NZ * ROWS, LANES), f32(LANES, LANES)],
            late_col, conduct_level, basin, owner_slot.reshape(2, LANES),
            geothermal, drag, surface_enthalpy, melt_level, ice_mask,
            places="asaaaaaaa" + "aa",
            scratch=(
                vmem(NZ * ROWS, LANES), vmem(5, ROWS, LANES),
                vmem(ROWS, LANES, dtype=jnp.int32), vmem(2, LANES, dtype=jnp.int32),
                vmem(ROWS, LANES, dtype=jnp.int32), vmem(LANES, LANES), dma((8,)), dma((3,)),
            ),
            limit=FULL,
        )
        basis, turned = call(
            basis_kernel, [f32(2, 3, ROWS, LANES), f32(2, 3, WIDE, LANES)],
            fields, west, east, south, rows, places="aaaaa" + "aa",
            scratch=(
                vmem(10, 8, LANES), vmem(2, 8, LANES), vmem(2, 8, LANES), vmem(8, 8, LANES),
                vmem(8, LANES), vmem(8, LANES), vmem(10, 8, LANES),
                vmem(2, 3, ROWS, LANES), vmem(2, 3, WIDE, LANES), dma((7,)),
            ),
            limit=FULL,
        )

    with jax.named_scope("transport"):
        reduced, velocity, send = call(
            main_kernel,
            [f32(NZ * ROWS, LANES), f32(2, ROWS, LANES), f32(LANES, LANES)],
            low, high, south, north, west, east,
            basis, turned, every, inv, plane, conduct_level,
            places="a" * 12 + "aaa",
            scratch=(
                vmem(2, 32, WIDE + 16, LANES), vmem(2, 32, BAND + 16, LANES),
                vmem(32, WIDE, LANES), vmem(32, WIDE, LANES),
                vmem(32, BAND, LANES), vmem(32, BAND, LANES),
                vmem(2, 32, WIDE, LANES), vmem(NZ * ROWS, LANES),
                vmem(32, 8, LANES), vmem(32, 8, LANES),
                vmem(2, 3, ROWS, LANES), vmem(2, 3, WIDE, LANES), vmem(LANES, LANES),
                vmem(NZ * ROWS, LANES), vmem(LANES, LANES), pltpu.SMEM((NZ,), jnp.float32),
                vmem(NZ * ROWS, LANES), vmem(2, ROWS, LANES), vmem(LANES, LANES),
                dma((26,)), dma((7,)),
            ),
            limit=FULL,
        )

    with jax.named_scope("basin_melt"):
        received = lax.all_to_all(send.reshape(LANES, 1, LANES), both, 0, 0)
        basin_melt = jnp.sum(received.reshape(LANES, LANES)[:, :2], axis=0)

    with jax.named_scope("substitution"):
        (solved,) = call(
            back_kernel, [f32(NZ * ROWS, LANES)],
            reduced, inv, enthalpy.reshape(NZ * ROWS, LANES), ice_mask, plane, conduct_level,
            places="vvvvvs" + "d",
        )
    return (solved.reshape(NZ, ROWS, LANES), velocity, basin_melt)


def solution(mesh):
    return jax.shard_map(
        per_device,
        mesh=mesh,
        in_specs=(
            P(None, "gy", "gx"),
            P("gy", "gx"),
            P(),
            P("gy", "gx"),
            P("gy", "gx"),
            P("gy", "gx"),
            P("gy", "gx"),
            P("gy", "gx"),
            P(None, "gy", "gx"),
            P("gy", "gx"),
            P("gy", "gx"),
            P(),
        ),
        out_specs=(P(None, "gy", "gx"), P(None, "gy", "gx"), P(("gx", "gy"))),
        check_vma=False,
    )
```

```python
import jax
import jax.numpy as jnp
from jax import lax
from jax.experimental import pallas as pl
from jax.experimental.pallas import tpu as pltpu
from jax.sharding import PartitionSpec as P

STEPS = 8
NZ = 160
ROWS = 16
LANES = 128
GROUPS = NZ // 8
SCALE = 16.0
WIDE = 144
BAND = 48
FULL = 63.4
MOST = 60
SMALL = 8
COPIES = 4


def lane_ids(shape):
    return lax.broadcasted_iota(jnp.int32, shape, len(shape) - 1)


def row_ids(shape):
    return lax.broadcasted_iota(jnp.int32, shape, len(shape) - 2)


def turn(x, shift, axis):
    shift = shift % x.shape[axis]
    return x if shift == 0 else pltpu.roll(x, shift, axis)


def f32(*shape):
    return jax.ShapeDtypeStruct(shape, jnp.float32)


def call(kernel, outs, *args, places, scratch=(), limit=8, cost=None, aliases={}):
    spaces = {"v": pltpu.VMEM, "s": pltpu.SMEM, "a": pltpu.HBM}
    specs = [
        pl.BlockSpec(memory_space=spaces[p]) if p in spaces else pl.BlockSpec()
        for p in places
    ]
    if cost is None:
        cost = sum(a.size * 4 for a in args) + sum(o.size * 4 for o in outs)
    return pl.pallas_call(
        kernel,
        out_shape=outs,
        in_specs=specs[: len(args)],
        out_specs=specs[len(args) :],
        scratch_shapes=list(scratch),
        input_output_aliases=aliases,
        compiler_params=pltpu.CompilerParams(vmem_limit_bytes=int(limit * 1024 * 1024)),
        cost_estimate=pl.CostEstimate(
            flops=0, bytes_accessed=cost, transcendentals=0
        ),
    )(*args)


def rows_at(start, size):
    return pl.ds(pl.multiple_of(start, size if size in (8, 16) else 8), size)


def stencil(visc, drag, keep_e, keep_w, keep_n, keep_s):
    wide = visc.shape[1]
    tall = visc.shape[0]
    east = 0.5 * (visc + turn(visc, -1, 1) * keep_e)
    west = 0.5 * (visc + turn(visc, 1, 1) * keep_w)
    north = 0.5 * (visc + turn(visc, -1, 0) * keep_n)
    south = 0.5 * (visc + turn(visc, 1, 0) * keep_s)
    center = drag + east + west + north + south
    inv = 1.0 / SCALE
    center, east, west, north, south = (
        center * inv,
        east * keep_e * inv,
        west * keep_w * inv,
        north * keep_n * inv,
        south * keep_s * inv,
    )

    def apply(w):
        return (
            center * w
            - east * turn(w, -1, 1)
            - west * turn(w, 1, 1)
            - north * turn(w, -1, 0)
            - south * turn(w, 1, 0)
        )

    return apply


def edge_tile(tiles, first):
    lane = lane_ids((8, LANES))
    out = jnp.zeros((8, LANES), jnp.float32)
    for i in range(8):
        x = turn(tiles[i], 16 * i if first else 16 * i - 112, 1)
        out = jnp.where((lane >= 16 * i) & (lane < 16 * i + 16), x, out)
    return out


def fetch_all(pairs, sems):
    copies = [
        pltpu.make_async_copy(src, dst, sems.at[i]) for i, (src, dst) in enumerate(pairs)
    ]
    for copy in copies:
        copy.start()
    return copies


def wait_all(copies):
    for copy in copies:
        copy.wait()


def fields_kernel(stress_ref, visc_ref, drag_ref, f_ref, raw, out, sems):
    pairs = [(stress_ref, raw.at[pl.ds(0, 2)]), (visc_ref, raw.at[2]), (drag_ref, raw.at[3])]
    wait_all(fetch_all(pairs, sems))
    tiles = [raw[i // 2, 8 * (i % 2) : 8 * (i % 2) + 8, :] for i in range(8)]
    for i in range(8):
        out[i] = tiles[i]
    out[8] = edge_tile(tiles, True)
    out[9] = edge_tile(tiles, False)
    wait_all(fetch_all([(out, f_ref)], sems))


LOW = 160
HIGH = 168


def transpose_kernel(
    e_ref, f_ref, lo_ref, hi_ref, first_ref, last_ref,
    buf, out, fields, first, last, in_sems, out_sems,
):
    loads = fetch_all(
        [(e_ref.at[:, pl.ds(8 * h, 8), :], buf.at[h]) for h in range(2)]
        + [(f_ref.at[pl.ds(0, 8)], fields)],
        in_sems,
    )
    stores = []

    def send(src, dst):
        copy = pltpu.make_async_copy(src, dst, out_sems.at[len(stores)])
        copy.start()
        stores.append(copy)

    for h, o_ref in ((0, lo_ref), (1, hi_ref)):
        loads[h].wait()
        for y in range(8):
            tiles = [buf[h, 8 * g : 8 * g + 8, y, :] for g in range(GROUPS)]
            wide = jnp.concatenate(tiles[:16], axis=0).T
            upper = jnp.concatenate(tiles[16:], axis=0)
            bands = jnp.concatenate([turn(upper, -32 * q, 1) for q in range(4)], axis=0)
            bands = bands.T[:32, :]
            out[h, y, :LANES, :] = wide
            out[h, y, LANES:, :] = bands
            first[8 * h + y] = wide[:8]
            last[8 * h + y] = wide[120:]
            first[16 + 8 * h + y] = bands[:8]
            last[16 + 8 * h + y] = bands[24:]
        send(out.at[h], o_ref.at[:, pl.ds(0, NZ), :])
    loads[2].wait()
    send(fields, hi_ref.at[:, pl.ds(NZ, 8), :])
    send(first, first_ref)
    send(last, last_ref)
    wait_all(stores)


def columns_kernel(
    own_first, own_last, f_hbm, y_hbm, s_hbm, n_hbm, first_ref, last_ref,
    mine, halo, fields, edges, out, sems, out_sems,
):
    pairs = [(own_first, mine.at[0]), (own_last, mine.at[1])]
    for i, msg in enumerate((s_hbm, n_hbm)):
        for j, at in enumerate((0, 120, 128, 152)):
            pairs.append((msg.at[:, pl.ds(at, 8), :], halo.at[i, j]))
    pairs.append((s_hbm.at[:, pl.ds(NZ, 8), :], fields))
    for i, ref in enumerate((f_hbm, y_hbm)):
        pairs.append((ref.at[pl.ds(8, 2)], edges.at[i]))
    wait_all(fetch_all(pairs, sems))
    lane = lane_ids((8, LANES))
    for side in range(2):
        for y in range(8):
            out[side, y] = halo[0, side, y]
            out[side, 24 + y] = halo[1, side, y]
        for y in range(16):
            out[side, 8 + y] = mine[side, y]
        for p in range(8):
            tile = None
            for j in range(4):
                y = 4 * p + j
                if y < 8:
                    x = halo[0, 2 + side, y]
                elif y < 24:
                    x = mine[side, 16 + y - 8]
                else:
                    x = halo[1, 2 + side, y - 24]
                x = turn(x, 32 * j - 96 * side, 1)
                tile = x if j == 0 else jnp.where(lane >= 32 * j, x, tile)
            out[side, 32 + p] = tile
        out[side, 40] = edge_tile([fields[i] for i in range(8)], side == 0)
        out[side, 41] = edges[0, side]
        out[side, 42] = edges[1, side]
    wait_all(fetch_all([(out.at[0], first_ref), (out.at[1], last_ref)], out_sems))


def edges_kernel(f_ref, y_ref, o_ref):
    o_ref[0] = f_ref[8]
    o_ref[1] = y_ref[8]


def moments_kernel(f_ref, y_ref, x_ref, o_ref):
    lane8 = lane_ids((8, LANES))
    fields = []
    for f in range(4):
        main = jnp.concatenate([f_ref[2 * f], f_ref[2 * f + 1], y_ref[2 * f]], axis=0)
        extra = [
            turn(x_ref[0], -16 * (2 * f), 1),
            turn(x_ref[0], -16 * (2 * f + 1), 1),
            turn(x_ref[1], -16 * (2 * f), 1),
        ]
        extra = [jnp.where(lane8 < 16, x, 0.0) for x in extra]
        fields.append(jnp.concatenate([main, jnp.concatenate(extra, axis=0)], axis=1))
    shape = fields[0].shape
    lane, row = lane_ids(shape), row_ids(shape)
    last_x = jnp.where(lax.axis_index("gx") == 7, 127, -9)
    last_y = jnp.where(lax.axis_index("gy") == 15, 15, -9)
    keep_e = jnp.where(lane == last_x, 0.0, 1.0)
    keep_w = jnp.where(lane == last_x + 1, 0.0, 1.0)
    keep_n = jnp.where(row == last_y, 0.0, 1.0)
    keep_s = jnp.where(row == last_y + 1, 0.0, 1.0)
    apply = stencil(fields[2], fields[3], keep_e, keep_w, keep_n, keep_s)
    inside = (row >= 3) & (row < 19) & (lane >= 3) & (lane < 131)
    v0 = fields[:2]
    v1 = [apply(w) for w in v0]
    v2 = [apply(w) for w in v1]
    v3 = [apply(w) for w in v2]
    result = jnp.zeros((1, LANES), jnp.float32)
    pairs = ((v0, v0), (v0, v1), (v1, v1), (v1, v2), (v2, v2), (v2, v3))
    for j, (p, q) in enumerate(pairs):
        prod = jnp.where(inside, p[0] * q[0] + p[1] * q[1], 0.0)
        part = prod[:, :LANES] + prod[:, LANES:]
        total = jnp.sum(jnp.sum(part, axis=0, keepdims=True), axis=1, keepdims=True)
        result = jnp.where(lane_ids((1, LANES)) == j, total, result)
    rows = row_ids((LANES * COPIES, LANES))
    o_ref[...] = jnp.where(rows % COPIES == 0, jnp.broadcast_to(result, rows.shape), 0.0)


def krylov_basis(own, west, east, south, north, o_ref, t_ref):
    lane8 = lane_ids((8, LANES))
    fields = []
    for f in range(4):
        main, extra = [], []
        for t in range(6):
            i = 2 * f + t % 2
            if t < 2:
                mid = south[i]
            elif t < 4:
                mid = own[i]
            else:
                mid = north[i]
            main.append(mid)
            right = turn(east[t // 2], -16 * i, 1)
            left = turn(west[t // 2], 112 - 16 * i, 1)
            extra.append(jnp.where(lane8 < 16, right, jnp.where(lane8 >= 112, left, 0.0)))
        fields.append(
            jnp.concatenate(
                [jnp.concatenate(main, axis=0), jnp.concatenate(extra, axis=0)], axis=1
            )
        )
    shape = fields[0].shape
    lane, row = lane_ids(shape), row_ids(shape)
    low_y = jnp.where(lax.axis_index("gy") == 0, 16, 0)
    high_y = jnp.where(lax.axis_index("gy") == 15, 32, 48)
    end_x = jnp.where(lax.axis_index("gx") == 7, 128, 144)
    start_x = jnp.where(lax.axis_index("gx") == 0, 256, 240)
    inside = (row >= low_y) & (row < high_y) & ((lane < end_x) | (lane >= start_x))
    inside = jnp.where(inside, 1.0, 0.0)
    fields = [x * inside for x in fields]
    apply = stencil(fields[2], fields[3], 1.0, 1.0, 1.0, 1.0)
    vectors = [fields[:2]]
    for _ in range(2):
        vectors.append([apply(w) * inside for w in vectors[-1]])
    fill = jnp.zeros((96, LANES), jnp.float32)
    for b in range(3):
        for c in range(2):
            v = vectors[b][c]
            o_ref[c, b] = v[16:32, :LANES]
            v = turn(v[8:40, :], 8, 1)
            t_ref[c, b, :LANES] = jnp.concatenate([v[:, :LANES], fill], axis=0).T
            t_ref[c, b, LANES:] = jnp.concatenate([v[:, LANES:], fill], axis=0).T[:16, :]


def cg_coefficients(m):
    a0 = m[0] / m[1]
    rr1 = a0 * a0 * m[2] - m[0]
    b0 = rr1 / m[0]
    p1 = (1.0 + b0, -a0)
    q1 = p1[0] * p1[0] * m[1] + 2.0 * p1[0] * p1[1] * m[2] + p1[1] * p1[1] * m[3]
    a1 = rr1 / q1
    r2 = (1.0, -a0 - a1 * p1[0], -a1 * p1[1])

    def form(p, k):
        return (
            p[0] * p[0] * m[k]
            + 2.0 * p[0] * p[1] * m[k + 1]
            + (2.0 * p[0] * p[2] + p[1] * p[1]) * m[k + 2]
            + 2.0 * p[1] * p[2] * m[k + 3]
            + p[2] * p[2] * m[k + 4]
        )

    rr2 = form(r2, 0)
    b1 = rr2 / rr1
    p2 = (1.0 + b1 * p1[0], r2[1] + b1 * p1[1], r2[2])
    a2 = rr2 / form(p2, 1)
    inv = 1.0 / SCALE
    return (
        (a0 + a1 * p1[0] + a2 * p2[0]) * inv,
        (a1 * p1[1] + a2 * p2[1]) * inv,
        a2 * p2[2] * inv,
    )


def main_kernel(
    lo_ref, hi_ref, s_ref, n_ref, w_ref, x_ref, f_ref, y_ref, sums_ref, lev_ref,
    col_ref, geo_ref, drag_ref, surf_ref, melt_ref, mask_ref, basin_ref, owner_ref, e_ref,
    o_ref, vel_ref, send_ref,
    wide, band, wide_x, wide_y, band_x, band_y, flow, adv,
    west_b, east_b, basis, turned, inv, planes, masks, owner, lev,
    own_f, west_f, east_f, south_f, north_f, solved, vel, send, old,
    sems, out_sems,
):
    lane8 = lane_ids((8, LANES))
    lane1 = lane_ids((1, LANES))
    copies = []

    def fetch(src, dst):
        copy = pltpu.make_async_copy(src, dst, sems.at[len(copies)])
        copy.start()
        copies.append(copy)
        return copy

    first = [
        fetch(f_ref, own_f), fetch(w_ref.at[pl.ds(40, 3)], west_f),
        fetch(x_ref.at[pl.ds(40, 3)], east_f), fetch(s_ref.at[:, pl.ds(NZ, 8), :], south_f),
        fetch(y_ref, north_f), fetch(lev_ref, lev), fetch(col_ref, planes.at[0]),
    ]
    field_here = []
    for i, ref in enumerate((s_ref, lo_ref, hi_ref, n_ref)):
        y = pl.ds(8 * i, 8)
        field_here.append(fetch(ref.at[:, pl.ds(0, 128), :], wide.at[0, y, pl.ds(16, 128), :]))
        field_here.append(fetch(ref.at[:, pl.ds(128, 32), :], band.at[0, y, pl.ds(16, 32), :]))
    for x, ref, buf in ((8, w_ref, west_b), (144, x_ref, east_b)):
        dst = wide.at[0, :, pl.ds(x, 8), :]
        field_here.append(fetch(ref.at[pl.ds(0, 32)], dst))
        field_here.append(fetch(ref.at[pl.ds(32, 8)], buf))
    later = [
        fetch(geo_ref, planes.at[1]), fetch(drag_ref, planes.at[2]),
        fetch(surf_ref, planes.at[3]), fetch(melt_ref, planes.at[4]),
        fetch(mask_ref, masks.at[0]), fetch(basin_ref, masks.at[1]), fetch(owner_ref, owner),
        fetch(e_ref, old),
    ]
    total = jnp.sum(sums_ref[...], axis=0, keepdims=True)
    m = [
        jnp.sum(jnp.where(lane1 == j, total, 0.0), axis=1, keepdims=True) for j in range(6)
    ]
    c = cg_coefficients(m)

    def profile(k):
        height = (k.astype(jnp.float32) + 0.5) / NZ
        low = 1.0 - height
        low = low * low
        return 1.0 - low * low

    prof_w = profile(lane8)
    prof_b = profile(128 + lane8 % 32)
    wait_all(first)
    col = planes[0]
    krylov_basis(own_f, west_f, east_f, south_f, north_f, basis, turned)

    def courants(i, s):
        for j in range(53):
            k = NZ - 1 - (i * 53 + j)
            lower = col * lev[k - 1]
            one = 1.0 / (s + lower)
            inv[rows_at(k * ROWS, ROWS), :] = one
            s = 1.0 + lower * (s * one)
        for j in range(6):
            at = rows_at((i * 6 + j) * 8, 8)
            for comp, o_ref in ((0, wide_x), (1, wide_y)):
                v = c[0] * turned[comp, 0, at, :]
                v = v + c[1] * turned[comp, 1, at, :]
                v = v + c[2] * turned[comp, 2, at, :]
                v = 3.0 * v
                for y in range(1, 31):
                    one = jnp.broadcast_to(v[:, y : y + 1], (8, LANES))
                    flow[comp, y, at, :] = one
                    o_ref[y, at, :] = 0.45 * jnp.tanh(one * prof_w)
        return s

    s = lax.fori_loop(0, 3, courants, 1.0 + col * lev[NZ - 1])
    inv[0:ROWS, :] = 1.0 / s

    def band_courants(i, carry):
        for j in range(3):
            t = i * 3 + j
            for comp, o_ref in ((0, band_x), (1, band_y)):
                for y in range(1, 31):
                    one = flow[comp, y, rows_at(t * 8, 8), :]
                    for q in range(1, 4):
                        other = flow[comp, y, rows_at(t * 8 + 32 * q, 8), :]
                        one = jnp.where(lane8 >= 32 * q, other, one)
                    o_ref[y, rows_at(t * 8, 8), :] = 0.45 * jnp.tanh(one * prof_b)
        return carry

    lax.fori_loop(0, 2, band_courants, 0)

    for comp in range(2):
        v = c[0] * basis[comp, 0] + c[1] * basis[comp, 1] + c[2] * basis[comp, 2]
        vel[comp] = v
    vel_out = pltpu.make_async_copy(vel, vel_ref, out_sems.at[0])
    vel_out.start()

    for copy in field_here:
        copy.wait()
    for y in range(32):
        left = turn(band[0, y, 40:48, :], 32, 1)
        left = jnp.where(lane8 < 32, turn(west_b[y // 4], -32 * (y % 4), 1), left)
        right = turn(band[0, y, 16:24, :], 96, 1)
        right = jnp.where(lane8 >= 96, turn(east_b[y // 4], 96 - 32 * (y % 4), 1), right)
        band[0, y, 8:16, :] = left
        band[0, y, 48:56, :] = right

    def substep(buf, cx_ref, cy_ref, s, t):
        src, dst = (s - 1) % 2, s % 2
        at = pl.multiple_of(t * 8, 8)
        mid = pl.ds(at + 8, 8)

        now = buf[src, s, mid, :]
        below = now - buf[src, s - 1, mid, :]
        for y in range(s, 32 - s):
            above = buf[src, y + 1, mid, :]
            west = buf[src, y, pl.ds(at + 7, 8), :]
            east = buf[src, y, pl.ds(at + 9, 8), :]
            cx = cx_ref[y, pl.ds(at, 8), :]
            cy = cy_ref[y, pl.ds(at, 8), :]
            rise = above - now
            across = jnp.where(cx > 0.0, now - west, east - now)
            along = jnp.where(cy > 0.0, below, rise)
            buf[dst, y, mid, :] = now - cx * across - cy * along
            now, below = above, rise

    for s in range(1, STEPS):

        def tiles(i, carry, s=s):
            for j in range(6):
                substep(wide, wide_x, wide_y, s, i * 6 + j)
            for j in range(2):
                substep(band, band_x, band_y, s, i * 2 + j)
            return carry

        lax.fori_loop(0, 3, tiles, 0)

    def last_step(buf, cx_ref, cy_ref, y, t):
        src, at = (STEPS - 1) % 2, 8 * t
        now = buf[src, y, at + 8 : at + 16, :]
        west = buf[src, y, at + 7 : at + 15, :]
        east = buf[src, y, at + 9 : at + 17, :]
        below = now - buf[src, y - 1, at + 8 : at + 16, :]
        rise = buf[src, y + 1, at + 8 : at + 16, :] - now
        cx = cx_ref[y, at : at + 8, :]
        cy = cy_ref[y, at : at + 8, :]
        across = jnp.where(cx > 0.0, now - west, east - now)
        return now - cx * across - cy * jnp.where(cy > 0.0, below, rise)

    def back(i, carry):
        for j in range(4):
            y = i * 4 + j
            x = [last_step(wide, wide_x, wide_y, y + 8, t) for t in range(1, 17)]
            x = jnp.concatenate(x, axis=0).T
            for g in range(16):
                adv[pl.ds(g * 128 + y, 8, stride=16), :] = x[8 * g : 8 * g + 8, :]
        x = [
            last_step(band, band_x, band_y, i * 4 + j + 8, t)
            for j in range(4)
            for t in range(1, 5)
        ]
        x = jnp.concatenate(x, axis=0).T
        for g in range(4):
            for j in range(4):
                out = None
                for q in range(4):
                    one = x[32 * q + 8 * g : 32 * q + 8 * g + 8, :]
                    one = turn(one, 32 * (q - j), 1)
                    out = one if q == 0 else jnp.where(lane8 >= 32 * q, one, out)
                adv[pl.ds((16 + g) * 128 + i * 4 + j, 8, stride=16), :] = out
        return carry

    lax.fori_loop(0, 4, back, 0)

    wait_all(later)

    def eliminate(i, above):
        k = NZ - 1 - i
        at = rows_at(k * ROWS, ROWS)
        one = inv[at, :]
        above = adv[at, :] * one + col * lev[k] * one * above
        solved[at, :] = above
        return above

    above = lax.fori_loop(0, NZ, eliminate, planes[3], unroll=16)
    u, v = vel[0], vel[1]
    bottom = planes[1] + 10.0 * planes[2] * (u * u + v * v)
    above = above + bottom * inv[0:ROWS, :]

    melt = jnp.where(masks[0] == 1, jnp.maximum(above - planes[4], 0.0), 0.0)
    melt = jnp.sum(melt, axis=0, keepdims=True) * MEAN
    place = row_ids((LANES, LANES)) * 2 + lane_ids((LANES, LANES))
    place = jnp.where(lane_ids((LANES, LANES)) < 2, place, -1)
    slots = owner[...]
    ids = row_ids(slots.shape) * LANES + lane_ids(slots.shape)
    out = jnp.zeros((LANES, LANES), jnp.float32)
    for j in range(4):
        part = jnp.where((lane1 >= 32 * j) & (lane1 < 32 * j + 32), melt, 0.0)
        part = jnp.sum(part, axis=1, keepdims=True)
        mine = jnp.sum(jnp.where(lane1 == 32 * j, masks[1, 0:1, :], 0), axis=1, keepdims=True)
        slot = jnp.where(ids == mine, slots, 0)
        slot = jnp.sum(jnp.sum(slot, axis=0, keepdims=True), axis=1, keepdims=True)
        out = out + jnp.where(place == slot, part, 0.0)
    send[...] = out
    send_out = pltpu.make_async_copy(send, send_ref, out_sems.at[1])
    send_out.start()

    outs = [vel_out, send_out]
    ice = masks[0] == 1
    solved[0:ROWS, :] = jnp.where(ice, above, old[0:ROWS, :])

    def substitute(k, below):
        at = rows_at(k * ROWS, ROWS)
        below = solved[at, :] + col * lev[k - 1] * inv[at, :] * below
        solved[at, :] = jnp.where(ice, below, old[at, :])
        return below

    below = above
    parts = 5
    size = NZ // parts
    for part in range(parts):
        first_k = part * size
        below = lax.fori_loop(max(first_k, 1), first_k + size, substitute, below, unroll=16)
        at = pl.ds(first_k * ROWS, size * ROWS)
        copy = pltpu.make_async_copy(solved.at[at], o_ref.at[at], out_sems.at[2 + part])
        copy.start()
        outs.append(copy)
    wait_all(outs)


def hand_on(v_ref, o_ref):
    o_ref[...] = v_ref[...]


MEAN = 256 / 262144


def per_device(
    enthalpy,
    conduct_col,
    conduct_level,
    surface_enthalpy,
    geothermal,
    melt_level,
    viscosity,
    drag,
    driving_stress,
    ice_mask,
    basin,
    owner_slot,
):
    nx, ny = lax.axis_size("gx"), lax.axis_size("gy")
    both = ("gx", "gy")
    up_x = [(i, i + 1) for i in range(nx - 1)]
    down_x = [(i + 1, i) for i in range(nx - 1)]
    ring_x = [((i + 1) % nx, i) for i in range(nx)]
    up_y = [(i, i + 1) for i in range(ny - 1)]
    down_y = [(i + 1, i) for i in range(ny - 1)]
    ring_y = [((i + 1) % ny, i) for i in range(ny)]
    dma = pltpu.SemaphoreType.DMA

    def vmem(*shape, dtype=jnp.float32):
        return pltpu.VMEM(shape, dtype)

    tie = lax.optimization_barrier

    with jax.named_scope("fields"):
        (fields,) = call(
            fields_kernel, [f32(10, 8, LANES)], driving_stress, viscosity, drag,
            places="aaa" + "a",
            scratch=(vmem(4, ROWS, LANES), vmem(10, 8, LANES), dma((3,))),
            limit=MOST,
        )
        rows = lax.ppermute(fields, "gy", ring_y)
    with jax.named_scope("levels_on_lanes"):
        low, high, first, last = call(
            transpose_kernel,
            [f32(8, LOW, LANES), f32(8, HIGH, LANES)] + [f32(32, 8, LANES)] * 2,
            enthalpy, fields, places="aa" + "aaaa",
            scratch=(
                vmem(2, NZ, 8, LANES), vmem(2, 8, NZ, LANES), vmem(8, 8, LANES),
                vmem(32, 8, LANES), vmem(32, 8, LANES), dma((3,)), dma((5,)),
            ),
            limit=FULL,
        )
    with jax.named_scope("moments"):
        (message,) = call(
            edges_kernel, [f32(2, 8, LANES)], fields, rows, places="vv" + "v", limit=SMALL
        )
        edge = lax.ppermute(message, "gx", ring_x)
        (sums,) = call(
            moments_kernel, [f32(LANES * COPIES, LANES)], fields, rows, edge, places="vvv" + "v",
            limit=SMALL,
        )

    with jax.named_scope("halo"):
        high_out, low_out, _ = tie((high, low, message))
        south = lax.ppermute(high_out, "gy", up_y)
        north = lax.ppermute(low_out, "gy", down_y)

    with jax.named_scope("moments"):
        every = lax.all_to_all(sums.reshape(LANES, COPIES, LANES), both, 0, 0)
        every = every.reshape(LANES * COPIES, LANES)

    with jax.named_scope("halo"):
        first, last, _ = tie((first, last, sums))
        first, last = call(
            columns_kernel, [f32(43, 8, LANES)] * 2,
            first, last, fields, rows, south, north, places="aaaaaa" + "aa",
            scratch=(
                vmem(2, 32, 8, LANES), vmem(2, 4, 8, 8, LANES), vmem(8, 8, LANES),
                vmem(2, 2, 8, LANES), vmem(2, 43, 8, LANES), dma((13,)), dma((2,)),
            ),
            limit=FULL, cost=0,
        )
        east = lax.ppermute(first, "gx", down_x)
        west = lax.ppermute(last, "gx", up_x)

    with jax.named_scope("transport"):
        solved, velocity, send = call(
            main_kernel,
            [f32(NZ * ROWS, LANES), f32(2, ROWS, LANES), f32(LANES, LANES)],
            low, high, south, north, west, east, fields, rows, every, conduct_level,
            conduct_col, geothermal, drag, surface_enthalpy, melt_level, ice_mask, basin,
            owner_slot.reshape(2, LANES), enthalpy.reshape(NZ * ROWS, LANES),
            places="aaaavvaa" + "v" + "a" * 10 + "aaa",
            scratch=(
                vmem(2, 32, WIDE + 16, LANES), vmem(2, 32, BAND + 16, LANES),
                vmem(32, WIDE, LANES), vmem(32, WIDE, LANES),
                vmem(32, BAND, LANES), vmem(32, BAND, LANES),
                vmem(2, 32, WIDE, LANES), vmem(NZ * ROWS, LANES),
                vmem(8, 8, LANES), vmem(8, 8, LANES),
                vmem(2, 3, ROWS, LANES), vmem(2, 3, WIDE, LANES),
                vmem(NZ * ROWS, LANES), vmem(5, ROWS, LANES),
                vmem(2, ROWS, LANES, dtype=jnp.int32), vmem(2, LANES, dtype=jnp.int32),
                pltpu.SMEM((NZ,), jnp.float32),
                vmem(10, 8, LANES), vmem(3, 8, LANES), vmem(3, 8, LANES), vmem(8, 8, LANES),
                vmem(10, 8, LANES),
                vmem(NZ * ROWS, LANES), vmem(2, ROWS, LANES), vmem(LANES, LANES),
                vmem(NZ * ROWS, LANES),
                dma((32,)), dma((8,)),
            ),
            limit=MOST,
        )

    with jax.named_scope("basin_melt"):
        received = lax.all_to_all(send.reshape(LANES, 1, LANES), both, 0, 0)
        basin_melt = jnp.sum(received.reshape(LANES, LANES)[:, :2], axis=0)
        (velocity,) = call(
            hand_on, [f32(2, ROWS, LANES)], velocity, places="vd", limit=SMALL, cost=1 << 23
        )

    return (solved.reshape(NZ, ROWS, LANES), velocity, basin_melt)


def solution(mesh):
    return jax.shard_map(
        per_device,
        mesh=mesh,
        in_specs=(
            P(None, "gy", "gx"),
            P("gy", "gx"),
            P(),
            P("gy", "gx"),
            P("gy", "gx"),
            P("gy", "gx"),
            P("gy", "gx"),
            P("gy", "gx"),
            P(None, "gy", "gx"),
            P("gy", "gx"),
            P("gy", "gx"),
            P(),
        ),
        out_specs=(P(None, "gy", "gx"), P(None, "gy", "gx"), P(("gx", "gy"))),
        check_vma=False,
    )
```

```python
import jax
import jax.numpy as jnp
from jax import lax
from jax.experimental import pallas as pl
from jax.experimental.pallas import tpu as pltpu
from jax.sharding import PartitionSpec as P

STEPS = 8
NZ = 160
ROWS = 16
LANES = 128
GROUPS = NZ // 8
SCALE = 16.0
WIDE = 144
BAND = 48
FULL = 63.4
MOST = 60
SMALL = 8
COPIES = 4


def lane_ids(shape):
    return lax.broadcasted_iota(jnp.int32, shape, len(shape) - 1)


def row_ids(shape):
    return lax.broadcasted_iota(jnp.int32, shape, len(shape) - 2)


def turn(x, shift, axis):
    shift = shift % x.shape[axis]
    return x if shift == 0 else pltpu.roll(x, shift, axis)


def f32(*shape):
    return jax.ShapeDtypeStruct(shape, jnp.float32)


def call(kernel, outs, *args, places, scratch=(), limit=8, cost=None, aliases={}):
    spaces = {"v": pltpu.VMEM, "s": pltpu.SMEM, "a": pltpu.HBM}
    specs = [
        pl.BlockSpec(memory_space=spaces[p]) if p in spaces else pl.BlockSpec()
        for p in places
    ]
    if cost is None:
        cost = sum(a.size * 4 for a in args) + sum(o.size * 4 for o in outs)
    return pl.pallas_call(
        kernel,
        out_shape=outs,
        in_specs=specs[: len(args)],
        out_specs=specs[len(args) :],
        scratch_shapes=list(scratch),
        input_output_aliases=aliases,
        compiler_params=pltpu.CompilerParams(vmem_limit_bytes=int(limit * 1024 * 1024)),
        cost_estimate=pl.CostEstimate(
            flops=0, bytes_accessed=cost, transcendentals=0
        ),
    )(*args)


def rows_at(start, size):
    return pl.ds(pl.multiple_of(start, size if size in (8, 16) else 8), size)


def stencil(visc, drag, keep_e, keep_w, keep_n, keep_s):
    wide = visc.shape[1]
    tall = visc.shape[0]
    east = 0.5 * (visc + turn(visc, -1, 1) * keep_e)
    west = 0.5 * (visc + turn(visc, 1, 1) * keep_w)
    north = 0.5 * (visc + turn(visc, -1, 0) * keep_n)
    south = 0.5 * (visc + turn(visc, 1, 0) * keep_s)
    center = drag + east + west + north + south
    inv = 1.0 / SCALE
    center, east, west, north, south = (
        center * inv,
        east * keep_e * inv,
        west * keep_w * inv,
        north * keep_n * inv,
        south * keep_s * inv,
    )

    def apply(w):
        return (
            center * w
            - east * turn(w, -1, 1)
            - west * turn(w, 1, 1)
            - north * turn(w, -1, 0)
            - south * turn(w, 1, 0)
        )

    return apply


def edge_tile(tiles, first):
    lane = lane_ids((8, LANES))
    out = jnp.zeros((8, LANES), jnp.float32)
    for i in range(8):
        x = turn(tiles[i], 16 * i if first else 16 * i - 112, 1)
        out = jnp.where((lane >= 16 * i) & (lane < 16 * i + 16), x, out)
    return out


def start_copy(src, dst, sem):
    if not isinstance(src, tuple) and not isinstance(dst, tuple):
        copy = pltpu.make_async_copy(src, dst, sem)
        copy.start()
        return copy
    src = src if isinstance(src, tuple) else (src, src)
    dst = dst if isinstance(dst, tuple) else (dst, dst)
    odd = lax.rem(lax.axis_index("gy"), 2)
    copies = [pltpu.make_async_copy(src[p], dst[p], sem) for p in range(2)]
    for p in range(2):

        @pl.when(odd == p)
        def _(p=p):
            copies[p].start()

    return copies[0]


def fetch_all(pairs, sems):
    return [start_copy(src, dst, sems.at[i]) for i, (src, dst) in enumerate(pairs)]


def wait_all(copies):
    for copy in copies:
        copy.wait()


def fields_kernel(stress_ref, visc_ref, drag_ref, f_ref, raw, out, sems):
    pairs = [(stress_ref, raw.at[pl.ds(0, 2)]), (visc_ref, raw.at[2]), (drag_ref, raw.at[3])]
    wait_all(fetch_all(pairs, sems))
    tiles = [raw[i // 2, 8 * (i % 2) : 8 * (i % 2) + 8, :] for i in range(8)]
    for i in range(8):
        out[i] = tiles[i]
    out[8] = edge_tile(tiles, True)
    out[9] = edge_tile(tiles, False)
    wait_all(fetch_all([(out, f_ref)], sems))


ALONG = 168


def transpose_kernel(
    e_ref, f_ref, one_ref, two_ref, first_ref, last_ref,
    buf, out, fields, first, last, in_sems, out_sems,
):
    loads = fetch_all(
        [(e_ref.at[:, pl.ds(8 * h, 8), :], buf.at[h]) for h in range(2)]
        + [(f_ref.at[pl.ds(0, 8)], fields)],
        in_sems,
    )
    stores = []

    def send(src, dst):
        stores.append(start_copy(src, dst, out_sems.at[len(stores)]))

    rows = [ref.at[:, pl.ds(0, NZ), :] for ref in (one_ref, two_ref)]
    for h in range(2):
        loads[h].wait()
        for y in range(8):
            tiles = [buf[h, 8 * g : 8 * g + 8, y, :] for g in range(GROUPS)]
            wide = jnp.concatenate(tiles[:16], axis=0).T
            upper = jnp.concatenate(tiles[16:], axis=0)
            bands = jnp.concatenate([turn(upper, -32 * q, 1) for q in range(4)], axis=0)
            bands = bands.T[:32, :]
            out[h, y, :LANES, :] = wide
            out[h, y, LANES:, :] = bands
            first[8 * h + y] = wide[:8]
            last[8 * h + y] = wide[120:]
            first[16 + 8 * h + y] = bands[:8]
            last[16 + 8 * h + y] = bands[24:]
        send(out.at[h], (rows[1 - h], rows[h]))
    loads[2].wait()
    send(fields, one_ref.at[:, pl.ds(NZ, 8), :])
    send(fields, two_ref.at[:, pl.ds(NZ, 8), :])
    send(first, first_ref)
    send(last, last_ref)
    wait_all(stores)


def columns_kernel(
    own_first, own_last, f_hbm, y_hbm, one_hbm, two_hbm, first_ref, last_ref,
    mine, halo, fields, edges, out, sems, out_sems,
):
    pairs = [(own_first, mine.at[0]), (own_last, mine.at[1])]
    south, north = (two_hbm, one_hbm), (one_hbm, two_hbm)

    def rows_of(pair, at):
        return tuple(msg.at[:, pl.ds(at, 8), :] for msg in pair)

    for i, pair in enumerate((south, north)):
        for j, at in enumerate((0, 120, 128, 152)):
            pairs.append((rows_of(pair, at), halo.at[i, j]))
    pairs.append((rows_of(south, NZ), fields))
    for i, ref in enumerate((f_hbm, y_hbm)):
        pairs.append((ref.at[pl.ds(8, 2)], edges.at[i]))
    wait_all(fetch_all(pairs, sems))
    lane = lane_ids((8, LANES))
    for side in range(2):
        for y in range(8):
            out[side, y] = halo[0, side, y]
            out[side, 24 + y] = halo[1, side, y]
        for y in range(16):
            out[side, 8 + y] = mine[side, y]
        for p in range(8):
            tile = None
            for j in range(4):
                y = 4 * p + j
                if y < 8:
                    x = halo[0, 2 + side, y]
                elif y < 24:
                    x = mine[side, 16 + y - 8]
                else:
                    x = halo[1, 2 + side, y - 24]
                x = turn(x, 32 * j - 96 * side, 1)
                tile = x if j == 0 else jnp.where(lane >= 32 * j, x, tile)
            out[side, 32 + p] = tile
        out[side, 40] = edge_tile([fields[i] for i in range(8)], side == 0)
        out[side, 41] = edges[0, side]
        out[side, 42] = edges[1, side]
    wait_all(fetch_all([(out.at[0], first_ref), (out.at[1], last_ref)], out_sems))


def edges_kernel(f_ref, y_ref, o_ref):
    o_ref[0] = f_ref[8]
    o_ref[1] = y_ref[8]


def moments_kernel(f_ref, y_ref, x_ref, o_ref):
    lane8 = lane_ids((8, LANES))
    fields = []
    for f in range(4):
        main = jnp.concatenate([f_ref[2 * f], f_ref[2 * f + 1], y_ref[2 * f]], axis=0)
        extra = [
            turn(x_ref[0], -16 * (2 * f), 1),
            turn(x_ref[0], -16 * (2 * f + 1), 1),
            turn(x_ref[1], -16 * (2 * f), 1),
        ]
        extra = [jnp.where(lane8 < 16, x, 0.0) for x in extra]
        fields.append(jnp.concatenate([main, jnp.concatenate(extra, axis=0)], axis=1))
    shape = fields[0].shape
    lane, row = lane_ids(shape), row_ids(shape)
    last_x = jnp.where(lax.axis_index("gx") == 7, 127, -9)
    last_y = jnp.where(lax.axis_index("gy") == 15, 15, -9)
    keep_e = jnp.where(lane == last_x, 0.0, 1.0)
    keep_w = jnp.where(lane == last_x + 1, 0.0, 1.0)
    keep_n = jnp.where(row == last_y, 0.0, 1.0)
    keep_s = jnp.where(row == last_y + 1, 0.0, 1.0)
    apply = stencil(fields[2], fields[3], keep_e, keep_w, keep_n, keep_s)
    inside = (row >= 3) & (row < 19) & (lane >= 3) & (lane < 131)
    v0 = fields[:2]
    v1 = [apply(w) for w in v0]
    v2 = [apply(w) for w in v1]
    v3 = [apply(w) for w in v2]
    result = jnp.zeros((1, LANES), jnp.float32)
    pairs = ((v0, v0), (v0, v1), (v1, v1), (v1, v2), (v2, v2), (v2, v3))
    for j, (p, q) in enumerate(pairs):
        prod = jnp.where(inside, p[0] * q[0] + p[1] * q[1], 0.0)
        part = prod[:, :LANES] + prod[:, LANES:]
        total = jnp.sum(jnp.sum(part, axis=0, keepdims=True), axis=1, keepdims=True)
        result = jnp.where(lane_ids((1, LANES)) == j, total, result)
    rows = row_ids((LANES * COPIES, LANES))
    o_ref[...] = jnp.where(rows % COPIES == 0, jnp.broadcast_to(result, rows.shape), 0.0)


def krylov_basis(own, west, east, south, north, o_ref, t_ref):
    lane8 = lane_ids((8, LANES))
    fields = []
    for f in range(4):
        main, extra = [], []
        for t in range(6):
            i = 2 * f + t % 2
            if t < 2:
                mid = south[i]
            elif t < 4:
                mid = own[i]
            else:
                mid = north[i]
            main.append(mid)
            right = turn(east[t // 2], -16 * i, 1)
            left = turn(west[t // 2], 112 - 16 * i, 1)
            extra.append(jnp.where(lane8 < 16, right, jnp.where(lane8 >= 112, left, 0.0)))
        fields.append(
            jnp.concatenate(
                [jnp.concatenate(main, axis=0), jnp.concatenate(extra, axis=0)], axis=1
            )
        )
    shape = fields[0].shape
    lane, row = lane_ids(shape), row_ids(shape)
    low_y = jnp.where(lax.axis_index("gy") == 0, 16, 0)
    high_y = jnp.where(lax.axis_index("gy") == 15, 32, 48)
    end_x = jnp.where(lax.axis_index("gx") == 7, 128, 144)
    start_x = jnp.where(lax.axis_index("gx") == 0, 256, 240)
    inside = (row >= low_y) & (row < high_y) & ((lane < end_x) | (lane >= start_x))
    inside = jnp.where(inside, 1.0, 0.0)
    fields = [x * inside for x in fields]
    apply = stencil(fields[2], fields[3], 1.0, 1.0, 1.0, 1.0)
    vectors = [fields[:2]]
    for _ in range(2):
        vectors.append([apply(w) * inside for w in vectors[-1]])
    fill = jnp.zeros((96, LANES), jnp.float32)
    for b in range(3):
        for c in range(2):
            v = vectors[b][c]
            o_ref[c, b] = v[16:32, :LANES]
            v = turn(v[8:40, :], 8, 1)
            t_ref[c, b, :LANES] = jnp.concatenate([v[:, :LANES], fill], axis=0).T
            t_ref[c, b, LANES:] = jnp.concatenate([v[:, LANES:], fill], axis=0).T[:16, :]


def cg_coefficients(m):
    a0 = m[0] / m[1]
    rr1 = a0 * a0 * m[2] - m[0]
    b0 = rr1 / m[0]
    p1 = (1.0 + b0, -a0)
    q1 = p1[0] * p1[0] * m[1] + 2.0 * p1[0] * p1[1] * m[2] + p1[1] * p1[1] * m[3]
    a1 = rr1 / q1
    r2 = (1.0, -a0 - a1 * p1[0], -a1 * p1[1])

    def form(p, k):
        return (
            p[0] * p[0] * m[k]
            + 2.0 * p[0] * p[1] * m[k + 1]
            + (2.0 * p[0] * p[2] + p[1] * p[1]) * m[k + 2]
            + 2.0 * p[1] * p[2] * m[k + 3]
            + p[2] * p[2] * m[k + 4]
        )

    rr2 = form(r2, 0)
    b1 = rr2 / rr1
    p2 = (1.0 + b1 * p1[0], r2[1] + b1 * p1[1], r2[2])
    a2 = rr2 / form(p2, 1)
    inv = 1.0 / SCALE
    return (
        (a0 + a1 * p1[0] + a2 * p2[0]) * inv,
        (a1 * p1[1] + a2 * p2[1]) * inv,
        a2 * p2[2] * inv,
    )


def main_kernel(
    own_one, own_two, one_ref, two_ref, w_ref, x_ref, f_ref, y_ref, sums_ref, lev_ref,
    col_ref, geo_ref, drag_ref, surf_ref, melt_ref, mask_ref, basin_ref, owner_ref, e_ref,
    o_ref, vel_ref, send_ref,
    wide, band, wide_x, wide_y, band_x, band_y, flow, adv,
    west_b, east_b, basis, turned, inv, planes, masks, owner, lev,
    own_f, west_f, east_f, south_f, north_f, solved, vel, send, old,
    sems, out_sems,
):
    lane8 = lane_ids((8, LANES))
    lane1 = lane_ids((1, LANES))
    copies = []

    def fetch(src, dst):
        copies.append(start_copy(src, dst, sems.at[len(copies)]))
        return copies[-1]

    def rows_of(pair, at, size):
        return tuple(msg.at[:, pl.ds(at, size), :] for msg in pair)

    south, north = (two_ref, one_ref), (one_ref, two_ref)
    low, high = (own_two, own_one), (own_one, own_two)

    first = [
        fetch(f_ref, own_f), fetch(w_ref.at[pl.ds(40, 3)], west_f),
        fetch(x_ref.at[pl.ds(40, 3)], east_f), fetch(rows_of(south, NZ, 8), south_f),
        fetch(y_ref, north_f), fetch(lev_ref, lev), fetch(col_ref, planes.at[0]),
    ]
    field_here = []
    for i, pair in enumerate((south, low, high, north)):
        y = pl.ds(8 * i, 8)
        field_here.append(fetch(rows_of(pair, 0, LANES), wide.at[0, y, pl.ds(16, LANES), :]))
        field_here.append(fetch(rows_of(pair, LANES, 32), band.at[0, y, pl.ds(16, 32), :]))
    for x, ref, buf in ((8, w_ref, west_b), (144, x_ref, east_b)):
        dst = wide.at[0, :, pl.ds(x, 8), :]
        field_here.append(fetch(ref.at[pl.ds(0, 32)], dst))
        field_here.append(fetch(ref.at[pl.ds(32, 8)], buf))
    later = [
        fetch(geo_ref, planes.at[1]), fetch(drag_ref, planes.at[2]),
        fetch(surf_ref, planes.at[3]), fetch(melt_ref, planes.at[4]),
        fetch(mask_ref, masks.at[0]), fetch(basin_ref, masks.at[1]), fetch(owner_ref, owner),
        fetch(e_ref, old),
    ]
    total = jnp.sum(sums_ref[...], axis=0, keepdims=True)
    m = [
        jnp.sum(jnp.where(lane1 == j, total, 0.0), axis=1, keepdims=True) for j in range(6)
    ]
    c = cg_coefficients(m)

    def profile(k):
        height = (k.astype(jnp.float32) + 0.5) / NZ
        low = 1.0 - height
        low = low * low
        return 1.0 - low * low

    prof_w = profile(lane8)
    prof_b = profile(128 + lane8 % 32)
    wait_all(first)
    col = planes[0]
    krylov_basis(own_f, west_f, east_f, south_f, north_f, basis, turned)

    def courants(i, s):
        for j in range(53):
            k = NZ - 1 - (i * 53 + j)
            lower = col * lev[k - 1]
            one = 1.0 / (s + lower)
            inv[rows_at(k * ROWS, ROWS), :] = one
            s = 1.0 + lower * (s * one)
        for j in range(6):
            at = rows_at((i * 6 + j) * 8, 8)
            for comp, o_ref in ((0, wide_x), (1, wide_y)):
                v = c[0] * turned[comp, 0, at, :]
                v = v + c[1] * turned[comp, 1, at, :]
                v = v + c[2] * turned[comp, 2, at, :]
                v = 3.0 * v
                for y in range(1, 31):
                    one = jnp.broadcast_to(v[:, y : y + 1], (8, LANES))
                    flow[comp, y, at, :] = one
                    o_ref[y, at, :] = 0.45 * jnp.tanh(one * prof_w)
        return s

    s = lax.fori_loop(0, 3, courants, 1.0 + col * lev[NZ - 1])
    inv[0:ROWS, :] = 1.0 / s

    def band_courants(i, carry):
        for j in range(3):
            t = i * 3 + j
            for comp, o_ref in ((0, band_x), (1, band_y)):
                for y in range(1, 31):
                    one = flow[comp, y, rows_at(t * 8, 8), :]
                    for q in range(1, 4):
                        other = flow[comp, y, rows_at(t * 8 + 32 * q, 8), :]
                        one = jnp.where(lane8 >= 32 * q, other, one)
                    o_ref[y, rows_at(t * 8, 8), :] = 0.45 * jnp.tanh(one * prof_b)
        return carry

    lax.fori_loop(0, 2, band_courants, 0)

    for comp in range(2):
        v = c[0] * basis[comp, 0] + c[1] * basis[comp, 1] + c[2] * basis[comp, 2]
        vel[comp] = v
    vel_out = pltpu.make_async_copy(vel, vel_ref, out_sems.at[0])
    vel_out.start()

    for copy in field_here:
        copy.wait()
    for axis, end, x, buf in (("gx", 0, 8, west_b), ("gx", 7, 144, east_b)):

        @pl.when(lax.axis_index(axis) == end)
        def _(x=x, buf=buf):
            wide[0, :, x : x + 8, :] = jnp.zeros((32, 8, LANES), jnp.float32)
            buf[...] = jnp.zeros((8, 8, LANES), jnp.float32)

    for y in range(32):
        left = turn(band[0, y, 40:48, :], 32, 1)
        left = jnp.where(lane8 < 32, turn(west_b[y // 4], -32 * (y % 4), 1), left)
        right = turn(band[0, y, 16:24, :], 96, 1)
        right = jnp.where(lane8 >= 96, turn(east_b[y // 4], 96 - 32 * (y % 4), 1), right)
        band[0, y, 8:16, :] = left
        band[0, y, 48:56, :] = right

    for end, y in ((0, 0), (15, 24)):

        @pl.when(lax.axis_index("gy") == end)
        def _(y=y):
            for j in range(8):
                wide[0, y + j, 8:152, :] = jnp.zeros((WIDE, LANES), jnp.float32)
                band[0, y + j, 8:56, :] = jnp.zeros((BAND, LANES), jnp.float32)

    def substep(buf, cx_ref, cy_ref, s, t):
        src, dst = (s - 1) % 2, s % 2
        at = pl.multiple_of(t * 8, 8)
        mid = pl.ds(at + 8, 8)

        now = buf[src, s, mid, :]
        below = now - buf[src, s - 1, mid, :]
        for y in range(s, 32 - s):
            above = buf[src, y + 1, mid, :]
            west = buf[src, y, pl.ds(at + 7, 8), :]
            east = buf[src, y, pl.ds(at + 9, 8), :]
            cx = cx_ref[y, pl.ds(at, 8), :]
            cy = cy_ref[y, pl.ds(at, 8), :]
            rise = above - now
            across = jnp.where(cx > 0.0, now - west, east - now)
            along = jnp.where(cy > 0.0, below, rise)
            buf[dst, y, mid, :] = now - cx * across - cy * along
            now, below = above, rise

    for s in range(1, STEPS):

        def tiles(i, carry, s=s):
            for j in range(6):
                substep(wide, wide_x, wide_y, s, i * 6 + j)
            for j in range(2):
                substep(band, band_x, band_y, s, i * 2 + j)
            return carry

        lax.fori_loop(0, 3, tiles, 0)

    def last_step(buf, cx_ref, cy_ref, y, t):
        src, at = (STEPS - 1) % 2, 8 * t
        now = buf[src, y, at + 8 : at + 16, :]
        west = buf[src, y, at + 7 : at + 15, :]
        east = buf[src, y, at + 9 : at + 17, :]
        below = now - buf[src, y - 1, at + 8 : at + 16, :]
        rise = buf[src, y + 1, at + 8 : at + 16, :] - now
        cx = cx_ref[y, at : at + 8, :]
        cy = cy_ref[y, at : at + 8, :]
        across = jnp.where(cx > 0.0, now - west, east - now)
        return now - cx * across - cy * jnp.where(cy > 0.0, below, rise)

    def back(i, carry):
        for j in range(4):
            y = i * 4 + j
            x = [last_step(wide, wide_x, wide_y, y + 8, t) for t in range(1, 17)]
            x = jnp.concatenate(x, axis=0).T
            for g in range(16):
                adv[pl.ds(g * 128 + y, 8, stride=16), :] = x[8 * g : 8 * g + 8, :]
        x = [
            last_step(band, band_x, band_y, i * 4 + j + 8, t)
            for j in range(4)
            for t in range(1, 5)
        ]
        x = jnp.concatenate(x, axis=0).T
        for g in range(4):
            for j in range(4):
                out = None
                for q in range(4):
                    one = x[32 * q + 8 * g : 32 * q + 8 * g + 8, :]
                    one = turn(one, 32 * (q - j), 1)
                    out = one if q == 0 else jnp.where(lane8 >= 32 * q, one, out)
                adv[pl.ds((16 + g) * 128 + i * 4 + j, 8, stride=16), :] = out
        return carry

    lax.fori_loop(0, 4, back, 0)

    wait_all(later)

    def eliminate(i, above):
        k = NZ - 1 - i
        at = rows_at(k * ROWS, ROWS)
        one = inv[at, :]
        above = adv[at, :] * one + col * lev[k] * one * above
        solved[at, :] = above
        return above

    above = lax.fori_loop(0, NZ, eliminate, planes[3], unroll=16)
    u, v = vel[0], vel[1]
    bottom = planes[1] + 10.0 * planes[2] * (u * u + v * v)
    above = above + bottom * inv[0:ROWS, :]

    melt = jnp.where(masks[0] == 1, jnp.maximum(above - planes[4], 0.0), 0.0)
    melt = jnp.sum(melt, axis=0, keepdims=True) * MEAN
    place = row_ids((LANES, LANES)) * 2 + lane_ids((LANES, LANES))
    place = jnp.where(lane_ids((LANES, LANES)) < 2, place, -1)
    slots = owner[...]
    ids = row_ids(slots.shape) * LANES + lane_ids(slots.shape)
    out = jnp.zeros((LANES, LANES), jnp.float32)
    for j in range(4):
        part = jnp.where((lane1 >= 32 * j) & (lane1 < 32 * j + 32), melt, 0.0)
        part = jnp.sum(part, axis=1, keepdims=True)
        mine = jnp.sum(jnp.where(lane1 == 32 * j, masks[1, 0:1, :], 0), axis=1, keepdims=True)
        slot = jnp.where(ids == mine, slots, 0)
        slot = jnp.sum(jnp.sum(slot, axis=0, keepdims=True), axis=1, keepdims=True)
        out = out + jnp.where(place == slot, part, 0.0)
    send[...] = out
    send_out = pltpu.make_async_copy(send, send_ref, out_sems.at[1])
    send_out.start()

    outs = [vel_out, send_out]
    ice = masks[0] == 1
    solved[0:ROWS, :] = jnp.where(ice, above, old[0:ROWS, :])

    def substitute(k, below):
        at = rows_at(k * ROWS, ROWS)
        below = solved[at, :] + col * lev[k - 1] * inv[at, :] * below
        solved[at, :] = jnp.where(ice, below, old[at, :])
        return below

    below = above
    parts = 5
    size = NZ // parts
    for part in range(parts):
        first_k = part * size
        below = lax.fori_loop(max(first_k, 1), first_k + size, substitute, below, unroll=16)
        at = pl.ds(first_k * ROWS, size * ROWS)
        copy = pltpu.make_async_copy(solved.at[at], o_ref.at[at], out_sems.at[2 + part])
        copy.start()
        outs.append(copy)
    wait_all(outs)


def hand_on(v_ref, o_ref):
    o_ref[...] = v_ref[...]


MEAN = 256 / 262144


def per_device(
    enthalpy,
    conduct_col,
    conduct_level,
    surface_enthalpy,
    geothermal,
    melt_level,
    viscosity,
    drag,
    driving_stress,
    ice_mask,
    basin,
    owner_slot,
):
    nx, ny = lax.axis_size("gx"), lax.axis_size("gy")
    both = ("gx", "gy")
    up_x = [(i, (i + 1) % nx) for i in range(nx)]
    ring_x = [((i + 1) % nx, i) for i in range(nx)]
    ring_y = [((i + 1) % ny, i) for i in range(ny)]
    dma = pltpu.SemaphoreType.DMA

    def vmem(*shape, dtype=jnp.float32):
        return pltpu.VMEM(shape, dtype)

    tie = lax.optimization_barrier

    with jax.named_scope("fields"):
        (fields,) = call(
            fields_kernel, [f32(10, 8, LANES)], driving_stress, viscosity, drag,
            places="aaa" + "a",
            scratch=(vmem(4, ROWS, LANES), vmem(10, 8, LANES), dma((3,))),
            limit=MOST,
        )
        rows = lax.ppermute(fields, "gy", ring_y)
    with jax.named_scope("levels_on_lanes"):
        own_one, own_two, first, last = call(
            transpose_kernel,
            [f32(8, ALONG, LANES)] * 2 + [f32(32, 8, LANES)] * 2,
            enthalpy, fields, places="aa" + "aaaa",
            scratch=(
                vmem(2, NZ, 8, LANES), vmem(2, 8, NZ, LANES), vmem(8, 8, LANES),
                vmem(32, 8, LANES), vmem(32, 8, LANES), dma((3,)), dma((6,)),
            ),
            limit=FULL,
        )
    with jax.named_scope("moments"):
        (message,) = call(
            edges_kernel, [f32(2, 8, LANES)], fields, rows, places="vv" + "v", limit=SMALL
        )
        edge = lax.ppermute(message, "gx", ring_x)
        (sums,) = call(
            moments_kernel, [f32(LANES * COPIES, LANES)], fields, rows, edge, places="vvv" + "v",
            limit=SMALL,
        )

    with jax.named_scope("halo"):
        one, two, _ = tie((own_one, own_two, message))
        one = lax.ppermute(one, "gy", [(i, i ^ 1) for i in range(ny)])
        ends = (0, ny - 1)
        two = lax.ppermute(
            two, "gy", [(i, i if i in ends else ((i + 1) ^ 1) - 1) for i in range(ny)]
        )

    with jax.named_scope("moments"):
        every = lax.all_to_all(sums.reshape(LANES, COPIES, LANES), both, 0, 0)
        every = every.reshape(LANES * COPIES, LANES)

    with jax.named_scope("halo"):
        first, last, _ = tie((first, last, sums))
        first, last = call(
            columns_kernel, [f32(43, 8, LANES)] * 2,
            first, last, fields, rows, one, two, places="aaaaaa" + "aa",
            scratch=(
                vmem(2, 32, 8, LANES), vmem(2, 4, 8, 8, LANES), vmem(8, 8, LANES),
                vmem(2, 2, 8, LANES), vmem(2, 43, 8, LANES), dma((13,)), dma((2,)),
            ),
            limit=FULL, cost=0,
        )
        east = lax.ppermute(first, "gx", ring_x)
        west = lax.ppermute(last, "gx", up_x)

    with jax.named_scope("transport"):
        solved, velocity, send = call(
            main_kernel,
            [f32(NZ * ROWS, LANES), f32(2, ROWS, LANES), f32(LANES, LANES)],
            own_one, own_two, one, two, west, east, fields, rows, every, conduct_level,
            conduct_col, geothermal, drag, surface_enthalpy, melt_level, ice_mask, basin,
            owner_slot.reshape(2, LANES), enthalpy.reshape(NZ * ROWS, LANES),
            places="aaaavvaa" + "v" + "a" * 10 + "aaa",
            scratch=(
                vmem(2, 32, WIDE + 16, LANES), vmem(2, 32, BAND + 16, LANES),
                vmem(32, WIDE, LANES), vmem(32, WIDE, LANES),
                vmem(32, BAND, LANES), vmem(32, BAND, LANES),
                vmem(2, 32, WIDE, LANES), vmem(NZ * ROWS, LANES),
                vmem(8, 8, LANES), vmem(8, 8, LANES),
                vmem(2, 3, ROWS, LANES), vmem(2, 3, WIDE, LANES),
                vmem(NZ * ROWS, LANES), vmem(5, ROWS, LANES),
                vmem(2, ROWS, LANES, dtype=jnp.int32), vmem(2, LANES, dtype=jnp.int32),
                pltpu.SMEM((NZ,), jnp.float32),
                vmem(10, 8, LANES), vmem(3, 8, LANES), vmem(3, 8, LANES), vmem(8, 8, LANES),
                vmem(10, 8, LANES),
                vmem(NZ * ROWS, LANES), vmem(2, ROWS, LANES), vmem(LANES, LANES),
                vmem(NZ * ROWS, LANES),
                dma((32,)), dma((8,)),
            ),
            limit=MOST,
        )

    with jax.named_scope("basin_melt"):
        received = lax.all_to_all(send.reshape(LANES, 1, LANES), both, 0, 0)
        basin_melt = jnp.sum(received.reshape(LANES, LANES)[:, :2], axis=0)
        (velocity,) = call(
            hand_on, [f32(2, ROWS, LANES)], velocity, places="vd", limit=SMALL, cost=1 << 23
        )

    return (solved.reshape(NZ, ROWS, LANES), velocity, basin_melt)


def solution(mesh):
    return jax.shard_map(
        per_device,
        mesh=mesh,
        in_specs=(
            P(None, "gy", "gx"),
            P("gy", "gx"),
            P(),
            P("gy", "gx"),
            P("gy", "gx"),
            P("gy", "gx"),
            P("gy", "gx"),
            P("gy", "gx"),
            P(None, "gy", "gx"),
            P("gy", "gx"),
            P("gy", "gx"),
            P(),
        ),
        out_specs=(P(None, "gy", "gx"), P(None, "gy", "gx"), P(("gx", "gy"))),
        check_vma=False,
    )
```

```python
import jax
import jax.numpy as jnp
from jax import lax
from jax.experimental import pallas as pl
from jax.experimental.pallas import tpu as pltpu
from jax.sharding import PartitionSpec as P

STEPS = 8
NZ = 160
ROWS = 16
LANES = 128
GROUPS = NZ // 8
SCALE = 16.0
WIDE = 144
BAND = 48
FULL = 63.4
MOST = 60
SMALL = 8
COPIES = 4


def lane_ids(shape):
    return lax.broadcasted_iota(jnp.int32, shape, len(shape) - 1)


def row_ids(shape):
    return lax.broadcasted_iota(jnp.int32, shape, len(shape) - 2)


def turn(x, shift, axis):
    shift = shift % x.shape[axis]
    return x if shift == 0 else pltpu.roll(x, shift, axis)


def f32(*shape):
    return jax.ShapeDtypeStruct(shape, jnp.float32)


def call(kernel, outs, *args, places, scratch=(), limit=8, cost=None, aliases={}):
    spaces = {"v": pltpu.VMEM, "s": pltpu.SMEM, "a": pltpu.HBM}
    specs = [
        pl.BlockSpec(memory_space=spaces[p]) if p in spaces else pl.BlockSpec()
        for p in places
    ]
    if cost is None:
        cost = sum(a.size * 4 for a in args) + sum(o.size * 4 for o in outs)
    return pl.pallas_call(
        kernel,
        out_shape=outs,
        in_specs=specs[: len(args)],
        out_specs=specs[len(args) :],
        scratch_shapes=list(scratch),
        input_output_aliases=aliases,
        compiler_params=pltpu.CompilerParams(vmem_limit_bytes=int(limit * 1024 * 1024)),
        cost_estimate=pl.CostEstimate(
            flops=0, bytes_accessed=cost, transcendentals=0
        ),
    )(*args)


def rows_at(start, size):
    return pl.ds(pl.multiple_of(start, size if size in (8, 16) else 8), size)


def stencil(visc, drag, keep_e, keep_w, keep_n, keep_s):
    wide = visc.shape[1]
    tall = visc.shape[0]
    east = 0.5 * (visc + turn(visc, -1, 1) * keep_e)
    west = 0.5 * (visc + turn(visc, 1, 1) * keep_w)
    north = 0.5 * (visc + turn(visc, -1, 0) * keep_n)
    south = 0.5 * (visc + turn(visc, 1, 0) * keep_s)
    center = drag + east + west + north + south
    inv = 1.0 / SCALE
    center, east, west, north, south = (
        center * inv,
        east * keep_e * inv,
        west * keep_w * inv,
        north * keep_n * inv,
        south * keep_s * inv,
    )

    def apply(w):
        return (
            center * w
            - east * turn(w, -1, 1)
            - west * turn(w, 1, 1)
            - north * turn(w, -1, 0)
            - south * turn(w, 1, 0)
        )

    return apply


def edge_tile(tiles, first):
    lane = lane_ids((8, LANES))
    out = jnp.zeros((8, LANES), jnp.float32)
    for i in range(8):
        x = turn(tiles[i], 16 * i if first else 16 * i - 112, 1)
        out = jnp.where((lane >= 16 * i) & (lane < 16 * i + 16), x, out)
    return out


def start_copy(src, dst, sem):
    if not isinstance(src, tuple) and not isinstance(dst, tuple):
        copy = pltpu.make_async_copy(src, dst, sem)
        copy.start()
        return copy
    src = src if isinstance(src, tuple) else (src, src)
    dst = dst if isinstance(dst, tuple) else (dst, dst)
    odd = lax.rem(lax.axis_index("gy"), 2)
    copies = [pltpu.make_async_copy(src[p], dst[p], sem) for p in range(2)]
    for p in range(2):

        @pl.when(odd == p)
        def _(p=p):
            copies[p].start()

    return copies[0]


def fetch_all(pairs, sems):
    return [start_copy(src, dst, sems.at[i]) for i, (src, dst) in enumerate(pairs)]


def wait_all(copies):
    for copy in copies:
        copy.wait()


def fields_kernel(stress_ref, visc_ref, drag_ref, f_ref, raw, out, sems):
    pairs = [(stress_ref, raw.at[pl.ds(0, 2)]), (visc_ref, raw.at[2]), (drag_ref, raw.at[3])]
    wait_all(fetch_all(pairs, sems))
    tiles = [raw[i // 2, 8 * (i % 2) : 8 * (i % 2) + 8, :] for i in range(8)]
    for i in range(8):
        out[i] = tiles[i]
    out[8] = edge_tile(tiles, True)
    out[9] = edge_tile(tiles, False)
    wait_all(fetch_all([(out, f_ref)], sems))


ALONG = 168


def transpose_kernel(
    e_ref, f_ref, one_ref, two_ref, first_ref, last_ref,
    buf, out, fields, first, last, in_sems, out_sems,
):
    loads = fetch_all(
        [(e_ref.at[:, pl.ds(8 * h, 8), :], buf.at[h]) for h in range(2)]
        + [(f_ref.at[pl.ds(0, 8)], fields)],
        in_sems,
    )
    stores = []

    def send(src, dst):
        stores.append(start_copy(src, dst, out_sems.at[len(stores)]))

    for h in range(2):
        loads[h].wait()
        for y in range(8):
            tiles = [buf[h, 8 * g : 8 * g + 8, y, :] for g in range(GROUPS)]
            wide = jnp.concatenate(tiles[:16], axis=0).T
            upper = jnp.concatenate(tiles[16:], axis=0)
            bands = jnp.concatenate([turn(upper, -32 * q, 1) for q in range(4)], axis=0)
            bands = bands.T[:32, :]
            out[h, y, :LANES, :] = wide
            out[h, y, LANES:, :] = bands
            first[8 * h + y] = wide[:8]
            last[8 * h + y] = wide[120:]
            first[16 + 8 * h + y] = bands[:8]
            last[16 + 8 * h + y] = bands[24:]
            if y % 2 == 1:
                at = pl.ds(y - 1, 2)
                dst = [ref.at[at, pl.ds(0, NZ), :] for ref in (one_ref, two_ref)]
                send(out.at[h, at], (dst[1 - h], dst[h]))
    loads[2].wait()
    send(fields, one_ref.at[:, pl.ds(NZ, 8), :])
    send(fields, two_ref.at[:, pl.ds(NZ, 8), :])
    send(first, first_ref)
    send(last, last_ref)
    wait_all(stores)


def columns_kernel(
    own_first, own_last, f_hbm, y_hbm, one_hbm, two_hbm, first_ref, last_ref,
    mine, halo, fields, edges, out, sems, out_sems,
):
    pairs = [(own_first, mine.at[0]), (own_last, mine.at[1])]
    south, north = (two_hbm, one_hbm), (one_hbm, two_hbm)

    def rows_of(pair, at):
        return tuple(msg.at[:, pl.ds(at, 8), :] for msg in pair)

    for i, pair in enumerate((south, north)):
        for j, at in enumerate((0, 120, 128, 152)):
            pairs.append((rows_of(pair, at), halo.at[i, j]))
    pairs.append((rows_of(south, NZ), fields))
    for i, ref in enumerate((f_hbm, y_hbm)):
        pairs.append((ref.at[pl.ds(8, 2)], edges.at[i]))
    wait_all(fetch_all(pairs, sems))
    lane = lane_ids((8, LANES))
    for side in range(2):
        for y in range(8):
            out[side, y] = halo[0, side, y]
            out[side, 24 + y] = halo[1, side, y]
        for y in range(16):
            out[side, 8 + y] = mine[side, y]
        for p in range(8):
            tile = None
            for j in range(4):
                y = 4 * p + j
                if y < 8:
                    x = halo[0, 2 + side, y]
                elif y < 24:
                    x = mine[side, 16 + y - 8]
                else:
                    x = halo[1, 2 + side, y - 24]
                x = turn(x, 32 * j - 96 * side, 1)
                tile = x if j == 0 else jnp.where(lane >= 32 * j, x, tile)
            out[side, 32 + p] = tile
        out[side, 40] = edge_tile([fields[i] for i in range(8)], side == 0)
        out[side, 41] = edges[0, side]
        out[side, 42] = edges[1, side]
    wait_all(fetch_all([(out.at[0], first_ref), (out.at[1], last_ref)], out_sems))


def edges_kernel(f_ref, y_ref, o_ref):
    o_ref[0] = f_ref[8]
    o_ref[1] = y_ref[8]


def moments_kernel(f_ref, y_ref, x_ref, o_ref):
    lane8 = lane_ids((8, LANES))
    fields = []
    for f in range(4):
        main = jnp.concatenate([f_ref[2 * f], f_ref[2 * f + 1], y_ref[2 * f]], axis=0)
        extra = [
            turn(x_ref[0], -16 * (2 * f), 1),
            turn(x_ref[0], -16 * (2 * f + 1), 1),
            turn(x_ref[1], -16 * (2 * f), 1),
        ]
        extra = [jnp.where(lane8 < 16, x, 0.0) for x in extra]
        fields.append(jnp.concatenate([main, jnp.concatenate(extra, axis=0)], axis=1))
    shape = fields[0].shape
    lane, row = lane_ids(shape), row_ids(shape)
    last_x = jnp.where(lax.axis_index("gx") == 7, 127, -9)
    last_y = jnp.where(lax.axis_index("gy") == 15, 15, -9)
    keep_e = jnp.where(lane == last_x, 0.0, 1.0)
    keep_w = jnp.where(lane == last_x + 1, 0.0, 1.0)
    keep_n = jnp.where(row == last_y, 0.0, 1.0)
    keep_s = jnp.where(row == last_y + 1, 0.0, 1.0)
    apply = stencil(fields[2], fields[3], keep_e, keep_w, keep_n, keep_s)
    inside = (row >= 3) & (row < 19) & (lane >= 3) & (lane < 131)
    v0 = fields[:2]
    v1 = [apply(w) for w in v0]
    v2 = [apply(w) for w in v1]
    v3 = [apply(w) for w in v2]
    result = jnp.zeros((1, LANES), jnp.float32)
    pairs = ((v0, v0), (v0, v1), (v1, v1), (v1, v2), (v2, v2), (v2, v3))
    for j, (p, q) in enumerate(pairs):
        prod = jnp.where(inside, p[0] * q[0] + p[1] * q[1], 0.0)
        part = prod[:, :LANES] + prod[:, LANES:]
        total = jnp.sum(jnp.sum(part, axis=0, keepdims=True), axis=1, keepdims=True)
        result = jnp.where(lane_ids((1, LANES)) == j, total, result)
    rows = row_ids((LANES * COPIES, LANES))
    o_ref[...] = jnp.where(rows % COPIES == 0, jnp.broadcast_to(result, rows.shape), 0.0)


def krylov_basis(own, west, east, south, north, o_ref, t_ref):
    lane8 = lane_ids((8, LANES))
    fields = []
    for f in range(4):
        main, extra = [], []
        for t in range(6):
            i = 2 * f + t % 2
            if t < 2:
                mid = south[i]
            elif t < 4:
                mid = own[i]
            else:
                mid = north[i]
            main.append(mid)
            right = turn(east[t // 2], -16 * i, 1)
            left = turn(west[t // 2], 112 - 16 * i, 1)
            extra.append(jnp.where(lane8 < 16, right, jnp.where(lane8 >= 112, left, 0.0)))
        fields.append(
            jnp.concatenate(
                [jnp.concatenate(main, axis=0), jnp.concatenate(extra, axis=0)], axis=1
            )
        )
    shape = fields[0].shape
    lane, row = lane_ids(shape), row_ids(shape)
    low_y = jnp.where(lax.axis_index("gy") == 0, 16, 0)
    high_y = jnp.where(lax.axis_index("gy") == 15, 32, 48)
    end_x = jnp.where(lax.axis_index("gx") == 7, 128, 144)
    start_x = jnp.where(lax.axis_index("gx") == 0, 256, 240)
    inside = (row >= low_y) & (row < high_y) & ((lane < end_x) | (lane >= start_x))
    inside = jnp.where(inside, 1.0, 0.0)
    fields = [x * inside for x in fields]
    apply = stencil(fields[2], fields[3], 1.0, 1.0, 1.0, 1.0)
    vectors = [fields[:2]]
    for _ in range(2):
        vectors.append([apply(w) * inside for w in vectors[-1]])
    fill = jnp.zeros((96, LANES), jnp.float32)
    for b in range(3):
        for c in range(2):
            v = vectors[b][c]
            o_ref[c, b] = v[16:32, :LANES]
            v = turn(v[8:40, :], 8, 1)
            t_ref[c, b, :LANES] = jnp.concatenate([v[:, :LANES], fill], axis=0).T
            t_ref[c, b, LANES:] = jnp.concatenate([v[:, LANES:], fill], axis=0).T[:16, :]


def cg_coefficients(m):
    a0 = m[0] / m[1]
    rr1 = a0 * a0 * m[2] - m[0]
    b0 = rr1 / m[0]
    p1 = (1.0 + b0, -a0)
    q1 = p1[0] * p1[0] * m[1] + 2.0 * p1[0] * p1[1] * m[2] + p1[1] * p1[1] * m[3]
    a1 = rr1 / q1
    r2 = (1.0, -a0 - a1 * p1[0], -a1 * p1[1])

    def form(p, k):
        return (
            p[0] * p[0] * m[k]
            + 2.0 * p[0] * p[1] * m[k + 1]
            + (2.0 * p[0] * p[2] + p[1] * p[1]) * m[k + 2]
            + 2.0 * p[1] * p[2] * m[k + 3]
            + p[2] * p[2] * m[k + 4]
        )

    rr2 = form(r2, 0)
    b1 = rr2 / rr1
    p2 = (1.0 + b1 * p1[0], r2[1] + b1 * p1[1], r2[2])
    a2 = rr2 / form(p2, 1)
    inv = 1.0 / SCALE
    return (
        (a0 + a1 * p1[0] + a2 * p2[0]) * inv,
        (a1 * p1[1] + a2 * p2[1]) * inv,
        a2 * p2[2] * inv,
    )


def main_kernel(
    own_one, own_two, one_ref, two_ref, w_ref, x_ref, f_ref, y_ref, sums_ref, lev_ref,
    col_ref, geo_ref, drag_ref, surf_ref, melt_ref, mask_ref, basin_ref, owner_ref, e_ref,
    o_ref, vel_ref, send_ref,
    wide, band, wide_x, wide_y, band_x, band_y, flow, adv,
    west_b, east_b, basis, turned, inv, planes, masks, owner, lev,
    own_f, west_f, east_f, south_f, north_f, solved, vel, send, old,
    sems, out_sems,
):
    lane8 = lane_ids((8, LANES))
    lane1 = lane_ids((1, LANES))
    copies = []

    def fetch(src, dst):
        copies.append(start_copy(src, dst, sems.at[len(copies)]))
        return copies[-1]

    def rows_of(pair, at, size):
        return tuple(msg.at[:, pl.ds(at, size), :] for msg in pair)

    south, north = (two_ref, one_ref), (one_ref, two_ref)
    low, high = (own_two, own_one), (own_one, own_two)

    first = [
        fetch(f_ref, own_f), fetch(w_ref.at[pl.ds(40, 3)], west_f),
        fetch(x_ref.at[pl.ds(40, 3)], east_f), fetch(rows_of(south, NZ, 8), south_f),
        fetch(y_ref, north_f), fetch(lev_ref, lev), fetch(col_ref, planes.at[0]),
    ]
    field_here = []
    for i, pair in enumerate((south, low, high, north)):
        y = pl.ds(8 * i, 8)
        field_here.append(fetch(rows_of(pair, 0, LANES), wide.at[0, y, pl.ds(16, LANES), :]))
        field_here.append(fetch(rows_of(pair, LANES, 32), band.at[0, y, pl.ds(16, 32), :]))
    for x, ref, buf in ((8, w_ref, west_b), (144, x_ref, east_b)):
        dst = wide.at[0, :, pl.ds(x, 8), :]
        field_here.append(fetch(ref.at[pl.ds(0, 32)], dst))
        field_here.append(fetch(ref.at[pl.ds(32, 8)], buf))
    later = [
        fetch(geo_ref, planes.at[1]), fetch(drag_ref, planes.at[2]),
        fetch(surf_ref, planes.at[3]), fetch(melt_ref, planes.at[4]),
        fetch(mask_ref, masks.at[0]), fetch(basin_ref, masks.at[1]), fetch(owner_ref, owner),
        fetch(e_ref, old),
    ]
    total = jnp.sum(sums_ref[...], axis=0, keepdims=True)
    m = [
        jnp.sum(jnp.where(lane1 == j, total, 0.0), axis=1, keepdims=True) for j in range(6)
    ]
    c = cg_coefficients(m)

    def profile(k):
        height = (k.astype(jnp.float32) + 0.5) / NZ
        low = 1.0 - height
        low = low * low
        return 1.0 - low * low

    prof_w = profile(lane8)
    prof_b = profile(128 + lane8 % 32)
    wait_all(first)
    col = planes[0]
    krylov_basis(own_f, west_f, east_f, south_f, north_f, basis, turned)

    def courants(i, s):
        for j in range(6):
            for p in range(9 * j, min(9 * j + 9, 53)):
                k = NZ - 1 - (i * 53 + p)
                lower = col * lev[k - 1]
                one = 1.0 / (s + lower)
                inv[rows_at(k * ROWS, ROWS), :] = one
                s = 1.0 + lower * (s * one)
            at = rows_at((i * 6 + j) * 8, 8)
            for comp, o_ref in ((0, wide_x), (1, wide_y)):
                v = c[0] * turned[comp, 0, at, :]
                v = v + c[1] * turned[comp, 1, at, :]
                v = v + c[2] * turned[comp, 2, at, :]
                v = 3.0 * v
                for y in range(1, 31):
                    one = jnp.broadcast_to(v[:, y : y + 1], (8, LANES))
                    flow[comp, y, at, :] = one
                    o_ref[y, at, :] = 0.45 * jnp.tanh(one * prof_w)
        return s

    s = lax.fori_loop(0, 3, courants, 1.0 + col * lev[NZ - 1])
    inv[0:ROWS, :] = 1.0 / s

    def band_courants(i, carry):
        for j in range(3):
            t = i * 3 + j
            for comp, o_ref in ((0, band_x), (1, band_y)):
                for y in range(1, 31):
                    one = flow[comp, y, rows_at(t * 8, 8), :]
                    for q in range(1, 4):
                        other = flow[comp, y, rows_at(t * 8 + 32 * q, 8), :]
                        one = jnp.where(lane8 >= 32 * q, other, one)
                    o_ref[y, rows_at(t * 8, 8), :] = 0.45 * jnp.tanh(one * prof_b)
        return carry

    lax.fori_loop(0, 2, band_courants, 0)

    for comp in range(2):
        v = c[0] * basis[comp, 0] + c[1] * basis[comp, 1] + c[2] * basis[comp, 2]
        vel[comp] = v
    vel_out = pltpu.make_async_copy(vel, vel_ref, out_sems.at[0])
    vel_out.start()

    for copy in field_here:
        copy.wait()
    for axis, end, x, buf in (("gx", 0, 8, west_b), ("gx", 7, 144, east_b)):

        @pl.when(lax.axis_index(axis) == end)
        def _(x=x, buf=buf):
            wide[0, :, x : x + 8, :] = jnp.zeros((32, 8, LANES), jnp.float32)
            buf[...] = jnp.zeros((8, 8, LANES), jnp.float32)

    for y in range(32):
        left = turn(band[0, y, 40:48, :], 32, 1)
        left = jnp.where(lane8 < 32, turn(west_b[y // 4], -32 * (y % 4), 1), left)
        right = turn(band[0, y, 16:24, :], 96, 1)
        right = jnp.where(lane8 >= 96, turn(east_b[y // 4], 96 - 32 * (y % 4), 1), right)
        band[0, y, 8:16, :] = left
        band[0, y, 48:56, :] = right

    for end, y in ((0, 0), (15, 24)):

        @pl.when(lax.axis_index("gy") == end)
        def _(y=y):
            for j in range(8):
                wide[0, y + j, 8:152, :] = jnp.zeros((WIDE, LANES), jnp.float32)
                band[0, y + j, 8:56, :] = jnp.zeros((BAND, LANES), jnp.float32)

    def substep(buf, cx_ref, cy_ref, s, t):
        src, dst = (s - 1) % 2, s % 2
        at = pl.multiple_of(t * 8, 8)
        mid = pl.ds(at + 8, 8)

        now = buf[src, s, mid, :]
        below = now - buf[src, s - 1, mid, :]
        for y in range(s, 32 - s):
            above = buf[src, y + 1, mid, :]
            west = buf[src, y, pl.ds(at + 7, 8), :]
            east = buf[src, y, pl.ds(at + 9, 8), :]
            cx = cx_ref[y, pl.ds(at, 8), :]
            cy = cy_ref[y, pl.ds(at, 8), :]
            rise = above - now
            across = jnp.where(cx > 0.0, now - west, east - now)
            along = jnp.where(cy > 0.0, below, rise)
            buf[dst, y, mid, :] = now - cx * across - cy * along
            now, below = above, rise

    for s in range(1, STEPS):

        def tiles(i, carry, s=s):
            for j in range(9):
                substep(wide, wide_x, wide_y, s, i * 9 + j)
            for j in range(3):
                substep(band, band_x, band_y, s, i * 3 + j)
            return carry

        lax.fori_loop(0, 2, tiles, 0)

    def last_step(buf, cx_ref, cy_ref, y, t):
        src, at = (STEPS - 1) % 2, 8 * t
        now = buf[src, y, at + 8 : at + 16, :]
        west = buf[src, y, at + 7 : at + 15, :]
        east = buf[src, y, at + 9 : at + 17, :]
        below = now - buf[src, y - 1, at + 8 : at + 16, :]
        rise = buf[src, y + 1, at + 8 : at + 16, :] - now
        cx = cx_ref[y, at : at + 8, :]
        cy = cy_ref[y, at : at + 8, :]
        across = jnp.where(cx > 0.0, now - west, east - now)
        return now - cx * across - cy * jnp.where(cy > 0.0, below, rise)

    def back(i, carry):
        for j in range(4):
            y = i * 4 + j
            x = [last_step(wide, wide_x, wide_y, y + 8, t) for t in range(1, 17)]
            x = jnp.concatenate(x, axis=0).T
            for g in range(16):
                adv[pl.ds(g * 128 + y, 8, stride=16), :] = x[8 * g : 8 * g + 8, :]
        x = [
            last_step(band, band_x, band_y, i * 4 + j + 8, t)
            for j in range(4)
            for t in range(1, 5)
        ]
        x = jnp.concatenate(x, axis=0).T
        for g in range(4):
            for j in range(4):
                out = None
                for q in range(4):
                    one = x[32 * q + 8 * g : 32 * q + 8 * g + 8, :]
                    one = turn(one, 32 * (q - j), 1)
                    out = one if q == 0 else jnp.where(lane8 >= 32 * q, one, out)
                adv[pl.ds((16 + g) * 128 + i * 4 + j, 8, stride=16), :] = out
        return carry

    lax.fori_loop(0, 4, back, 0)

    wait_all(later)

    def eliminate(i, above):
        k = NZ - 1 - i
        at = rows_at(k * ROWS, ROWS)
        one = inv[at, :]
        above = adv[at, :] * one + col * lev[k] * one * above
        solved[at, :] = above
        return above

    above = lax.fori_loop(0, NZ, eliminate, planes[3], unroll=16)
    u, v = vel[0], vel[1]
    bottom = planes[1] + 10.0 * planes[2] * (u * u + v * v)
    above = above + bottom * inv[0:ROWS, :]

    melt = jnp.where(masks[0] == 1, jnp.maximum(above - planes[4], 0.0), 0.0)
    melt = jnp.sum(melt, axis=0, keepdims=True) * MEAN
    place = row_ids((LANES, LANES)) * 2 + lane_ids((LANES, LANES))
    place = jnp.where(lane_ids((LANES, LANES)) < 2, place, -1)
    slots = owner[...]
    ids = row_ids(slots.shape) * LANES + lane_ids(slots.shape)
    out = jnp.zeros((LANES, LANES), jnp.float32)
    for j in range(4):
        part = jnp.where((lane1 >= 32 * j) & (lane1 < 32 * j + 32), melt, 0.0)
        part = jnp.sum(part, axis=1, keepdims=True)
        mine = jnp.sum(jnp.where(lane1 == 32 * j, masks[1, 0:1, :], 0), axis=1, keepdims=True)
        slot = jnp.where(ids == mine, slots, 0)
        slot = jnp.sum(jnp.sum(slot, axis=0, keepdims=True), axis=1, keepdims=True)
        out = out + jnp.where(place == slot, part, 0.0)
    send[...] = out
    send_out = pltpu.make_async_copy(send, send_ref, out_sems.at[1])
    send_out.start()

    outs = [vel_out, send_out]
    ice = masks[0] == 1
    solved[0:ROWS, :] = jnp.where(ice, above, old[0:ROWS, :])

    def substitute(k, below):
        at = rows_at(k * ROWS, ROWS)
        below = solved[at, :] + col * lev[k - 1] * inv[at, :] * below
        solved[at, :] = jnp.where(ice, below, old[at, :])
        return below

    below = above
    parts = 5
    size = NZ // parts
    for part in range(parts):
        first_k = part * size
        below = lax.fori_loop(max(first_k, 1), first_k + size, substitute, below, unroll=16)
        at = pl.ds(first_k * ROWS, size * ROWS)
        copy = pltpu.make_async_copy(solved.at[at], o_ref.at[at], out_sems.at[2 + part])
        copy.start()
        outs.append(copy)
    wait_all(outs)


def hand_on(v_ref, o_ref):
    o_ref[...] = v_ref[...]


MEAN = 256 / 262144


def per_device(
    enthalpy,
    conduct_col,
    conduct_level,
    surface_enthalpy,
    geothermal,
    melt_level,
    viscosity,
    drag,
    driving_stress,
    ice_mask,
    basin,
    owner_slot,
):
    nx, ny = lax.axis_size("gx"), lax.axis_size("gy")
    both = ("gx", "gy")
    up_x = [(i, (i + 1) % nx) for i in range(nx)]
    ring_x = [((i + 1) % nx, i) for i in range(nx)]
    ring_y = [((i + 1) % ny, i) for i in range(ny)]
    dma = pltpu.SemaphoreType.DMA

    def vmem(*shape, dtype=jnp.float32):
        return pltpu.VMEM(shape, dtype)

    tie = lax.optimization_barrier

    with jax.named_scope("fields"):
        (fields,) = call(
            fields_kernel, [f32(10, 8, LANES)], driving_stress, viscosity, drag,
            places="aaa" + "a",
            scratch=(vmem(4, ROWS, LANES), vmem(10, 8, LANES), dma((3,))),
            limit=MOST,
        )
        rows = lax.ppermute(fields, "gy", ring_y)
    with jax.named_scope("levels_on_lanes"):
        own_one, own_two, first, last = call(
            transpose_kernel,
            [f32(8, ALONG, LANES)] * 2 + [f32(32, 8, LANES)] * 2,
            enthalpy, fields, places="aa" + "aaaa",
            scratch=(
                vmem(2, NZ, 8, LANES), vmem(2, 8, NZ, LANES), vmem(8, 8, LANES),
                vmem(32, 8, LANES), vmem(32, 8, LANES), dma((3,)), dma((12,)),
            ),
            limit=FULL,
        )
    with jax.named_scope("moments"):
        (message,) = call(
            edges_kernel, [f32(2, 8, LANES)], fields, rows, places="vv" + "v", limit=SMALL
        )
        edge = lax.ppermute(message, "gx", ring_x)
        (sums,) = call(
            moments_kernel, [f32(LANES * COPIES, LANES)], fields, rows, edge, places="vvv" + "v",
            limit=SMALL,
        )

    with jax.named_scope("halo"):
        one, two, _ = tie((own_one, own_two, message))
        one = lax.ppermute(one, "gy", [(i, i ^ 1) for i in range(ny)])
        ends = (0, ny - 1)
        two = lax.ppermute(
            two, "gy", [(i, i if i in ends else ((i + 1) ^ 1) - 1) for i in range(ny)]
        )

    with jax.named_scope("moments"):
        every = lax.all_to_all(sums.reshape(LANES, COPIES, LANES), both, 0, 0)
        every = every.reshape(LANES * COPIES, LANES)

    with jax.named_scope("halo"):
        first, last, _ = tie((first, last, sums))
        first, last = call(
            columns_kernel, [f32(43, 8, LANES)] * 2,
            first, last, fields, rows, one, two, places="aaaaaa" + "aa",
            scratch=(
                vmem(2, 32, 8, LANES), vmem(2, 4, 8, 8, LANES), vmem(8, 8, LANES),
                vmem(2, 2, 8, LANES), vmem(2, 43, 8, LANES), dma((13,)), dma((2,)),
            ),
            limit=FULL, cost=0,
        )
        east = lax.ppermute(first, "gx", ring_x)
        west = lax.ppermute(last, "gx", up_x)

    with jax.named_scope("transport"):
        solved, velocity, send = call(
            main_kernel,
            [f32(NZ * ROWS, LANES), f32(2, ROWS, LANES), f32(LANES, LANES)],
            own_one, own_two, one, two, west, east, fields, rows, every, conduct_level,
            conduct_col, geothermal, drag, surface_enthalpy, melt_level, ice_mask, basin,
            owner_slot.reshape(2, LANES), enthalpy.reshape(NZ * ROWS, LANES),
            places="aaaavvaa" + "v" + "a" * 10 + "aaa",
            scratch=(
                vmem(2, 32, WIDE + 16, LANES), vmem(2, 32, BAND + 16, LANES),
                vmem(32, WIDE, LANES), vmem(32, WIDE, LANES),
                vmem(32, BAND, LANES), vmem(32, BAND, LANES),
                vmem(2, 32, WIDE, LANES), vmem(NZ * ROWS, LANES),
                vmem(8, 8, LANES), vmem(8, 8, LANES),
                vmem(2, 3, ROWS, LANES), vmem(2, 3, WIDE, LANES),
                vmem(NZ * ROWS, LANES), vmem(5, ROWS, LANES),
                vmem(2, ROWS, LANES, dtype=jnp.int32), vmem(2, LANES, dtype=jnp.int32),
                pltpu.SMEM((NZ,), jnp.float32),
                vmem(10, 8, LANES), vmem(3, 8, LANES), vmem(3, 8, LANES), vmem(8, 8, LANES),
                vmem(10, 8, LANES),
                vmem(NZ * ROWS, LANES), vmem(2, ROWS, LANES), vmem(LANES, LANES),
                vmem(NZ * ROWS, LANES),
                dma((32,)), dma((8,)),
            ),
            limit=MOST,
        )

    with jax.named_scope("basin_melt"):
        received = lax.all_to_all(send.reshape(LANES, 1, LANES), both, 0, 0)
        basin_melt = jnp.sum(received.reshape(LANES, LANES)[:, :2], axis=0)
        (velocity,) = call(
            hand_on, [f32(2, ROWS, LANES)], velocity, places="vd", limit=SMALL, cost=1 << 23
        )

    return (solved.reshape(NZ, ROWS, LANES), velocity, basin_melt)


def solution(mesh):
    return jax.shard_map(
        per_device,
        mesh=mesh,
        in_specs=(
            P(None, "gy", "gx"),
            P("gy", "gx"),
            P(),
            P("gy", "gx"),
            P("gy", "gx"),
            P("gy", "gx"),
            P("gy", "gx"),
            P("gy", "gx"),
            P(None, "gy", "gx"),
            P("gy", "gx"),
            P("gy", "gx"),
            P(),
        ),
        out_specs=(P(None, "gy", "gx"), P(None, "gy", "gx"), P(("gx", "gy"))),
        check_vma=False,
    )
```
